512 devices in a mesh: seq: 128 (over z, y, core), head: 4 (over x).
Axes of the slice: x: 4, y: 8, z: 8, core: 2. Of those that a mesh axis runs over, the one named last changes fastest.
Arguments:
- activations: bfloat16 [65536, 1536], P('seq', 'head'), may hold values from -6 to 6
- owners: int32 [256], P('seq'), may hold values from 0 to 127, as said below
- owner_slot: int32 [256], P('seq'), may hold values from 0 to 1, as said below
- counts: int32 [256], P('seq'), may hold values from 1 to 256, as said below
- stale_pairs: bfloat16 [2, 65536, 1536], P(None, 'seq', 'head'), may hold values from -136 to 136
- w_query: bfloat16 [1536, 1536], P(None, 'head'), may hold values from -0.15625 to 0.15625
- w_out: bfloat16 [1536, 1536], P('head'), may hold values from -0.15625 to 0.15625
Outputs:
- mixed: bfloat16 [65536, 1536], P('seq', 'head')
The draws below stay inside these ranges and needn't reach their ends.
Inputs may be any that keep to these rules, and one draw needn't show every extreme that they name: Window j of device s goes to device owners = (s + o_k) mod 128 with k = owner_slot, for offsets o_k of 1 to 128 - 1 common to all devices, o_0 = 128 - 1; each device receives exactly 2 windows, one in each slot 0 to 1. `owner_slot`: the slots of one device's windows are distinct. `counts`: the first window holds 256 live tokens.
All inputs are finite; a program needn't handle non-finite values.
Results may differ from the reference program's by a relative error of at most 0.03.
Values may be sent and summed in bfloat16 or wider, within the bound.
A program may use at most 64 MiB of HBM per device.

```python
import jax
import jax.numpy as jnp
from jax import lax

HEADS = 24
HEAD_DIM = 64
D = 1536
WIN_DEV = 2
WSLOT = 256
WINDOWS = 256
TOK = 65536
N_SEQ = 128
N_HEAD = 4


def route_tables(key):
    offsets = jax.random.randint(jax.random.fold_in(key, 11), (WIN_DEV,), 1, N_SEQ).astype(jnp.int32)
    offsets = offsets.at[0].set(N_SEQ - 1)
    device_keys = jax.random.split(jax.random.fold_in(key, 12), N_SEQ)
    orders = jax.vmap(lambda sub_key: jax.random.permutation(sub_key, WIN_DEV))(device_keys).astype(jnp.int32)
    sources = jnp.arange(N_SEQ, dtype=jnp.int32)[:, None]
    targets = (sources + offsets[orders]) % N_SEQ
    return (targets.reshape(-1).astype(jnp.int32), orders.reshape(-1).astype(jnp.int32))


def draw_owners(key, part):
    tables = route_tables(key)
    return tables[0]


def draw_owner_slot(key, part):
    tables = route_tables(key)
    return tables[1]


def draw_counts(key, part):
    key = jax.random.fold_in(key, 7)
    drawn = jax.random.randint(key, (WINDOWS,), 1, WSLOT + 1).astype(jnp.int32)
    return drawn.at[0].set(WSLOT)


def draw_stale_pairs(key, part):
    key = jax.random.fold_in(key, 5)
    base_key = jax.random.fold_in(key, 0)
    shift_key = jax.random.fold_in(key, 2)
    factor = jnp.array([4.0, 1.0], jnp.float32)[:, None, None]
    shift_scale = jnp.array([3.2, 1.0], jnp.float32)[:, None, None, None]
    window_shift = jnp.clip(jax.random.normal(shift_key, (2, WINDOWS, 1, D), jnp.float32), -2.5, 2.5) * shift_scale
    window_shift = jnp.broadcast_to(window_shift, (2, WINDOWS, WSLOT, D)).reshape(2, TOK, D)
    base = jnp.clip(jax.random.normal(base_key, (2, TOK, D), jnp.float32), -6.0, 6.0)
    return (base * factor + window_shift).astype(jnp.bfloat16)


def level_of(rng, extent, cuts, least, largest):
    gain, own = 1.0, jax.random.fold_in(rng, 6)
    for position, parts in cuts:
        steps = jnp.exp(jax.random.uniform(jax.random.fold_in(own, position), (parts,), jnp.float32, least / len(cuts), largest / len(cuts)))
        gain = gain * jnp.repeat(steps, extent[position] // parts).reshape([-1 if axis == position else 1 for axis in range(len(extent))])
    return gain


def noise(key, extent, deviation, bound, shards=(), held_as=jnp.bfloat16):
    values = jax.random.normal(key, extent, jnp.float32) * deviation
    if len(shards) > 0:
        values = level_of(key, extent, shards, -0.22, 0.18) * values
    return jnp.clip(values, min=-bound, max=bound).astype(held_as)


def setup_inputs(seed: int = 0) -> dict:
    seeds = jax.random.split(jax.random.key(seed), 8)
    activations = noise(seeds[0], (TOK, D), 1.0, 6.0, ((0, 128), (1, 4)))
    owners = draw_owners(jax.random.fold_in(seeds[7], 71), 0)
    owner_slot = draw_owner_slot(jax.random.fold_in(seeds[7], 71), 0)
    counts = draw_counts(jax.random.fold_in(seeds[7], 71), 0)
    stale_pairs = draw_stale_pairs(jax.random.fold_in(seeds[7], 71), 0)
    w_query = noise(seeds[5], (D, D), D ** -0.5, 0.15625, ((1, 4),))
    w_out = noise(seeds[6], (D, D), D ** -0.5, 0.15625, ((0, 4),))
    return {"activations": activations, "owners": owners, "owner_slot": owner_slot, "counts": counts, "stale_pairs": stale_pairs, "w_query": w_query, "w_out": w_out}


def reference(activations, owners, owner_slot, counts, stale_pairs, w_query, w_out):
    attn_scale = HEAD_DIM ** -0.5
    highest = lax.Precision.HIGHEST
    windowed = activations.reshape(WINDOWS, WSLOT, D)
    target = (owners * WIN_DEV + owner_slot).astype(jnp.int32)
    moved = jnp.zeros_like(windowed).at[target].set(windowed).reshape(TOK, D)
    query = jnp.dot(moved, w_query, preferred_element_type=jnp.float32).astype(jnp.bfloat16)
    query_float = query.astype(jnp.float32).reshape(WINDOWS, WSLOT, HEADS, HEAD_DIM)
    key_tiles = stale_pairs[0].astype(jnp.float32).reshape(WINDOWS, WSLOT, HEADS, HEAD_DIM)
    value_tiles = stale_pairs[1].astype(jnp.float32).reshape(WINDOWS, WSLOT, HEADS, HEAD_DIM)
    live_slot = jnp.arange(WSLOT, dtype=jnp.int32)[None, :] < counts[:, None]
    live_weight = live_slot.astype(jnp.float32)[:, :, None, None]
    divisor = counts.astype(jnp.float32)[:, None, None]
    pooled_key = (jnp.sum(key_tiles * live_weight, axis=1) / divisor).astype(jnp.bfloat16)
    pooled_value = (jnp.sum(value_tiles * live_weight, axis=1) / divisor).astype(jnp.bfloat16)

    def fine_window(operands):
        window_query, window_key, window_value, window_live = operands
        scores = jnp.einsum("qhd,khd->hqk", window_query, window_key, precision=highest) * attn_scale
        scores = jnp.where(window_live[None, None, :], scores, -jnp.inf)
        probs = jax.nn.softmax(scores, axis=-1).astype(jnp.bfloat16).astype(jnp.float32)
        return jnp.einsum("hqk,khd->qhd", probs, window_value, precision=highest)

    fine_out = lax.map(fine_window, (query_float, key_tiles, value_tiles, live_slot))
    fine_out = fine_out.reshape(TOK, HEADS, HEAD_DIM)
    key_pool = pooled_key.astype(jnp.float32)
    value_pool = pooled_value.astype(jnp.float32)

    def coarse_block(block_query):
        block_scores = jnp.einsum("qhd,khd->hqk", block_query, key_pool, precision=highest) * attn_scale
        top_score = jnp.max(block_scores, axis=-1, keepdims=True)
        expo_weight = jnp.exp(block_scores - top_score)
        weight_sum = jnp.sum(expo_weight, axis=-1)
        summed_values = jnp.einsum("hqk,khd->qhd", expo_weight, value_pool, precision=highest)
        return summed_values / jnp.transpose(weight_sum)[:, :, None]

    coarse_out = lax.map(coarse_block, query_float.reshape(N_SEQ, WIN_DEV * WSLOT, HEADS, HEAD_DIM))
    coarse_out = coarse_out.reshape(TOK, HEADS, HEAD_DIM)
    attended = (fine_out + coarse_out).astype(jnp.bfloat16).reshape(TOK, D)
    group_cols = D // N_HEAD
    projected = jnp.zeros((TOK, D), jnp.float32)
    for head_group in range(N_HEAD):
        lower = head_group * group_cols
        part_sum = jnp.dot(attended[:, lower:lower + group_cols], w_out[lower:lower + group_cols], preferred_element_type=jnp.float32)
        rounded = lax.optimization_barrier(part_sum.astype(jnp.bfloat16))
        projected = projected + rounded.astype(jnp.float32)
    return (moved.astype(jnp.float32) + projected).astype(jnp.bfloat16)
```

```python
import functools

import jax
import jax.numpy as jnp
from jax import lax
from jax.experimental import pallas as pl
from jax.experimental.pallas import tpu as pltpu
from jax.sharding import PartitionSpec as P

HEAD_DIM = 64
PAIR = 2 * HEAD_DIM
Y_CHIPS = 8
CHUNK = 128
MESH = pl.DeviceIdType.MESH
F32 = jnp.float32
BF16 = jnp.bfloat16


def attention_kernel(
    seq_count,
    rows,
    counts,
    first,
    second,
    stale_hbm,
    wq_hbm,
    wo_hbm,
    out,
    xg,
    stale,
    wq,
    wo,
    stage,
    pool,
    pool_wide,
    kcat,
    vaug,
    q_s,
    att_s,
    p_opp,
    p_right,
    p_left,
    p_own,
    in_opp_left,
    in_opp_right,
    in_left,
    in_right,
    load_sem,
    x_send,
    x_recv,
    rs_send,
    rs_recv,
    pool_send,
    pool_recv,
):
    width = xg.shape[2]
    total = xg.shape[1]
    chunks = total // CHUNK
    half = CHUNK // 2
    pairs = width // PAIR
    per_window = rows // CHUNK
    z_chips = seq_count // (2 * Y_CHIPS)
    seq = lax.axis_index("seq")
    head = lax.axis_index("head")
    heads = lax.axis_size("head")
    core = lax.rem(seq, 2)
    y = lax.rem(lax.div(seq, 2), Y_CHIPS)
    z = lax.div(seq, 2 * Y_CHIPS)
    right = (seq, lax.rem(head + 1, heads))
    left = (seq, lax.rem(head + heads - 1, heads))
    other_core = (seq + 1 - 2 * core, head)
    inner = y + core * (z - y)
    outer = z + core * (y - z)
    inner_step = 2 + core * (2 * Y_CHIPS - 2)
    outer_step = 2 * Y_CHIPS - core * (2 * Y_CHIPS - 2)
    ring = z_chips

    def inner_peer(j):
        return (seq + (lax.rem(inner + j, ring) - inner) * inner_step, head)

    def outer_peer(j):
        return (seq + (lax.rem(outer + j, ring) - outer) * outer_step, head)

    loads = [
        pltpu.make_async_copy(stale_hbm, stale, load_sem.at[0]),
        pltpu.make_async_copy(wq_hbm, wq, load_sem.at[1]),
        pltpu.make_async_copy(wo_hbm, wo, load_sem.at[2]),
        pltpu.make_async_copy(first, xg.at[0, pl.ds(0, rows)], load_sem.at[3]),
        pltpu.make_async_copy(second, xg.at[0, pl.ds(rows, rows)], load_sem.at[4]),
    ]
    loads[0].start()
    loads[3].start()
    loads[4].start()
    loads[1].start()
    loads[2].start()

    barrier = pltpu.get_barrier_semaphore()
    peers = [left, right, other_core]
    peers += [inner_peer(j) for j in range(1, ring)]
    peers += [outer_peer(j) for j in range(1, ring)]
    for peer in peers:
        pl.semaphore_signal(barrier, inc=1, device_id=peer, device_id_type=MESH)
    pl.semaphore_wait(barrier, len(peers))

    def remote(src, dst, send, recv, peer):
        return pltpu.make_async_remote_copy(
            src_ref=src,
            dst_ref=dst,
            send_sem=send,
            recv_sem=recv,
            device_id=peer,
            device_id_type=MESH,
        )

    def direct(c, src, way):
        peer, slot = ((right, 1), (left, 3))[way]
        return remote(
            src,
            xg.at[slot, pl.ds(c * CHUNK, CHUNK)],
            x_send.at[way, c],
            x_recv.at[way, c],
            peer,
        )

    def forward(c, way):
        peer, slot = ((right, 1), (left, 3))[way]
        part = pl.ds(pl.multiple_of(c * CHUNK + way * half, half), half)
        return remote(
            xg.at[slot, part],
            xg.at[2, part],
            x_send.at[2 + way, c],
            x_recv.at[2 + way, c],
            peer,
        )

    sent = []
    for c in range(chunks):
        ref, at = (first, c) if c < per_window else (second, c - per_window)
        for way in range(2):
            copy = direct(c, ref.at[pl.ds(at * CHUNK, CHUNK)], way)
            copy.start()
            sent.append(copy)

    loads[0].wait()
    stage[...] = jnp.zeros_like(stage)
    row_ids = lax.broadcasted_iota(jnp.int32, (rows, width), 0)
    for kind in range(2):
        for w in range(2):
            count = counts[w]
            part = stale[kind, pl.ds(w * rows, rows), :].astype(F32)
            part = jnp.where(row_ids < count, part, 0.0)
            mean = jnp.sum(part, axis=0, keepdims=True) / count.astype(F32)
            for t in range(pairs):
                at = (kind * 2 + w) * pairs + t
                stage[pl.ds(at, 1), :] = mean[:, t * PAIR : (t + 1) * PAIR]
    pool[core, outer, inner] = stage[...].astype(BF16)

    def inner_copy(j, which):
        ref = pool.at[core, outer, which]
        return remote(ref, ref, pool_send.at[j - 1], pool_recv.at[j - 1], inner_peer(j))

    def outer_copy(j, which):
        ref = pool.at[core, which]
        at = ring + j - 2
        return remote(ref, ref, pool_send.at[at], pool_recv.at[at], outer_peer(j))

    def core_copy(which):
        ref = pool.at[which]
        at = 2 * ring - 2
        return remote(ref, ref, pool_send.at[at], pool_recv.at[at], other_core)

    for j in range(1, ring):
        inner_copy(j, inner).start()

    lanes = lax.broadcasted_iota(jnp.int32, (1, PAIR), 1)
    keep = [
        jnp.where(lanes < HEAD_DIM, 1.0, 0.0),
        jnp.where(lanes < HEAD_DIM, 0.0, 1.0),
    ]

    def lay_out(at, p, key, value):
        for which in range(2):
            part = pl.ds(which * rows, rows)
            kcat[at, p, part, :] = (key * keep[which]).astype(BF16)
            vaug[at, p, part, 0:PAIR] = (value * keep[which]).astype(BF16)
            vaug[at, p, part, PAIR : 2 * PAIR] = jnp.broadcast_to(
                keep[which], (rows, PAIR)
            ).astype(BF16)

    for w in range(2):
        for p in range(pairs):
            cols = slice(p * PAIR, (p + 1) * PAIR)
            lay_out(
                w,
                p,
                stale[0, pl.ds(w * rows, rows), cols].astype(F32),
                stale[1, pl.ds(w * rows, rows), cols].astype(F32),
            )

    def pass_on(c):
        for way in range(2):
            direct(c, xg.at[0, pl.ds(c * CHUNK, CHUNK)], way).wait_recv()
            forward(c, way).start()

    pass_on(0)

    for j in range(1, ring):
        inner_copy(j, lax.rem(inner + ring - j, ring)).wait_recv()
    for j in range(1, ring):
        outer_copy(j, outer).start()

    loads[1].wait()
    loads[2].wait()
    loads[3].wait()
    loads[4].wait()

    for j in range(1, ring):
        outer_copy(j, lax.rem(outer + ring - j, ring)).wait_recv()
    core_copy(core).start()
    pass_on(1)
    core_copy(1 - core).wait_recv()

    for i in range(2):
        for j in range(ring):
            at = (i * ring + j) * ring * 16
            pool_wide[pl.ds(at, ring * 16), :] = (
                pool[i, j].reshape(ring * 16, PAIR).astype(F32)
            )
    for p in range(pairs):
        pooled = []
        for kind in range(2):
            pieces = [
                pool_wide[pl.ds((kind * 2 + w) * pairs + p, seq_count, stride=16), :]
                for w in range(2)
            ]
            pooled.append(jnp.concatenate(pieces, axis=0))
        lay_out(2, p, pooled[0], pooled[1])

    def opp_copy(c, way):
        peer = (right, left)[way]
        dst = (in_opp_left, in_opp_right)[way]
        part = pl.ds(way * half, half)
        return remote(
            p_opp.at[c, part], dst.at[c], rs_send.at[way, c], rs_recv.at[way, c], peer
        )

    def share_copy(c, way, piece):
        peer = (right, left)[way]
        src = (p_right, p_left)[way]
        dst = (in_left, in_right)[way]
        part = pl.ds(piece * half, half)
        at = 2 + 2 * way + piece
        return remote(
            src.at[c, part], dst.at[c, part], rs_send.at[at, c], rs_recv.at[at, c], peer
        )

    def relay(c):
        for way in range(2):
            opp_copy(c, way).wait_recv()
            src = (p_right, p_left)[way]
            add = (in_opp_left, in_opp_right)[way]
            part = pl.ds(way * half, half)
            src[c, part, :] = (src[c, part, :].astype(F32) + add[c].astype(F32)).astype(BF16)
            share_copy(c, way, way).start()

    def softmax_out(at, p, query, bias):
        scores = lax.dot_general(
            query, kcat[at, p], (((1,), (1,)), ((), ())), preferred_element_type=F32
        )
        parts = []
        for which in range(2):
            part = scores[:, which * rows : (which + 1) * rows]
            if bias is not None:
                part = part + bias
            top = jnp.max(part, axis=1, keepdims=True)
            parts.append(jnp.exp(part - top).astype(BF16))
        both = jnp.dot(
            jnp.concatenate(parts, axis=1), vaug[at, p], preferred_element_type=F32
        )
        return both[:, 0:PAIR] / both[:, PAIR : 2 * PAIR]

    def step(c, carry):
        @pl.when(jnp.logical_and(c >= 1, c + 1 < chunks))
        def _():
            pass_on(c + 1)

        for way in range(2):
            forward(c, way).wait_recv()
        here = pl.ds(pl.multiple_of(c * CHUNK, CHUNK), CHUNK)
        query = None
        for r in range(4):
            source = lax.rem(head + heads - r, heads)
            w_rows = pl.ds(pl.multiple_of(source * width, width), width)
            term = jnp.dot(xg[r, here, :], wq[w_rows, :], preferred_element_type=F32)
            query = term if query is None else query + term
        q_s[...] = (query.astype(BF16).astype(F32) * HEAD_DIM ** (-0.5)).astype(BF16)
        w = lax.div(c, per_window)
        slots = lax.broadcasted_iota(jnp.int32, (1, rows), 1)
        bias = jnp.where(slots < counts[w], 0.0, -1e30)

        def pair(p, inner_carry):
            cols = pl.ds(pl.multiple_of(p * PAIR, PAIR), PAIR)
            q_p = q_s[:, cols]
            fine = softmax_out(w, p, q_p, bias)
            coarse = softmax_out(2, p, q_p, None)
            att_s[:, cols] = (fine + coarse).astype(BF16)
            return inner_carry

        lax.fori_loop(0, pairs, pair, 0)

        def project(r):
            target = lax.rem(head + r, heads)
            cols = pl.ds(pl.multiple_of(target * width, PAIR), width)
            return jnp.dot(att_s[...], wo[:, cols], preferred_element_type=F32).astype(BF16)

        p_opp[c] = project(2)
        opp_copy(c, 0).start()
        opp_copy(c, 1).start()
        p_right[c] = project(1)
        share_copy(c, 0, 1).start()
        p_left[c] = project(3)
        share_copy(c, 1, 0).start()
        p_own[c] = project(0)

        @pl.when(c >= 1)
        def _():
            relay(c - 1)

        return carry

    lax.fori_loop(0, chunks, step, 0)
    relay(chunks - 1)

    def finish(c, carry):
        for way in range(2):
            for piece in range(2):
                share_copy(c, way, piece).wait_recv()
        here = pl.ds(pl.multiple_of(c * CHUNK, CHUNK), CHUNK)
        projected = (
            p_own[c].astype(F32) + in_left[c].astype(F32) + in_right[c].astype(F32)
        )
        out[here, :] = (xg[0, here, :].astype(F32) + projected).astype(BF16)
        return carry

    lax.fori_loop(0, chunks, finish, 0)

    for copy in sent:
        copy.wait_send()
    for c in range(chunks):
        for way in range(2):
            forward(c, way).wait_send()
            opp_copy(c, way).wait_send()
            for piece in range(2):
                share_copy(c, way, piece).wait_send()
    for j in range(1, ring):
        inner_copy(j, inner).wait_send()
        outer_copy(j, outer).wait_send()
    core_copy(core).wait_send()


def on_device(activations, owners, owner_slot, counts, stale_pairs, w_query, w_out):
    seq_count = lax.axis_size("seq")
    total, width = activations.shape
    rows = total // owners.shape[0]
    chunks = total // CHUNK
    half = CHUNK // 2
    pairs = width // PAIR
    ring = Y_CHIPS
    in_order = owner_slot[0] == 0
    slot_0 = jnp.where(in_order, activations[:rows], activations[rows:])
    slot_1 = jnp.where(in_order, activations[rows:], activations[:rows])
    owner_1 = jnp.where(in_order, owners[1], owners[0])
    offset = (owner_1 - lax.axis_index("seq")) % seq_count

    def shift(value, by):
        return lax.ppermute(
            value, "seq", [(i, (i + by) % seq_count) for i in range(seq_count)]
        )

    first = shift(slot_0, seq_count - 1)
    second = lax.switch(
        offset - 1,
        [functools.partial(shift, by=by) for by in range(1, seq_count)],
        slot_1,
    )
    hbm = pl.BlockSpec(memory_space=pl.ANY)
    dma = pltpu.SemaphoreType.DMA
    return pl.pallas_call(
        functools.partial(attention_kernel, seq_count, rows),
        out_shape=jax.ShapeDtypeStruct((total, width), BF16),
        in_specs=[pl.BlockSpec(memory_space=pltpu.SMEM)] + [hbm] * 5,
        out_specs=pl.BlockSpec(memory_space=pltpu.VMEM),
        scratch_shapes=[
            pltpu.VMEM((4, total, width), BF16),
            pltpu.VMEM(stale_pairs.shape, BF16),
            pltpu.VMEM(w_query.shape, BF16),
            pltpu.VMEM(w_out.shape, BF16),
            pltpu.VMEM((16, PAIR), F32),
            pltpu.VMEM((2, ring, ring, 16, PAIR), BF16),
            pltpu.VMEM((2 * ring * ring * 16, PAIR), F32),
            pltpu.VMEM((3, pairs, 2 * rows, PAIR), BF16),
            pltpu.VMEM((3, pairs, 2 * rows, 2 * PAIR), BF16),
            pltpu.VMEM((CHUNK, width), BF16),
            pltpu.VMEM((CHUNK, width), BF16),
            pltpu.VMEM((chunks, CHUNK, width), BF16),
            pltpu.VMEM((chunks, CHUNK, width), BF16),
            pltpu.VMEM((chunks, CHUNK, width), BF16),
            pltpu.VMEM((chunks, CHUNK, width), BF16),
            pltpu.VMEM((chunks, half, width), BF16),
            pltpu.VMEM((chunks, half, width), BF16),
            pltpu.VMEM((chunks, CHUNK, width), BF16),
            pltpu.VMEM((chunks, CHUNK, width), BF16),
            dma((5,)),
            dma((4, chunks)),
            dma((4, chunks)),
            dma((6, chunks)),
            dma((6, chunks)),
            dma((2 * ring - 1,)),
            dma((2 * ring - 1,)),
        ],
        compiler_params=pltpu.CompilerParams(
            collective_id=0, has_side_effects=True, vmem_limit_bytes=40 * 1024 * 1024
        ),
        name="window_attention",
    )(counts, first, second, stale_pairs, w_query, w_out)


def solution(mesh):
    placed = (
        P("seq", "head"),
        P("seq"),
        P("seq"),
        P("seq"),
        P(None, "seq", "head"),
        P(None, "head"),
        P("head", None),
    )
    return jax.shard_map(
        on_device, mesh=mesh, in_specs=placed, out_specs=P("seq", "head"), check_vma=False
    )
```

```python
import functools

import jax
import jax.numpy as jnp
from jax import lax
from jax.experimental import pallas as pl
from jax.experimental.pallas import tpu as pltpu
from jax.sharding import PartitionSpec as P

HEAD_DIM = 64
PAIR = 2 * HEAD_DIM
Y_CHIPS = 8
CHUNK = 128
MESH = pl.DeviceIdType.MESH
F32 = jnp.float32
BF16 = jnp.bfloat16


def attention_kernel(
    seq_count,
    rows,
    owners,
    owner_slot,
    counts,
    act_hbm,
    stale_hbm,
    wq_hbm,
    wo_hbm,
    out,
    act,
    moving,
    landing,
    xg,
    stale,
    wq,
    wo,
    stage,
    pool,
    pool_wide,
    kcat,
    vaug,
    q_s,
    fine_s,
    att_s,
    p_opp,
    p_right,
    p_left,
    p_own,
    in_opp_left,
    in_opp_right,
    in_left,
    in_right,
    load_sem,
    home_send,
    home_recv,
    move_send,
    move_recv,
    x_send,
    x_recv,
    rs_send,
    rs_recv,
    pool_send,
    pool_recv,
):
    width = xg.shape[2]
    total = xg.shape[1]
    chunks = total // CHUNK
    half = CHUNK // 2
    pairs = width // PAIR
    per_window = rows // CHUNK
    z_chips = seq_count // (2 * Y_CHIPS)
    seq = lax.axis_index("seq")
    head = lax.axis_index("head")
    heads = lax.axis_size("head")
    core = lax.rem(seq, 2)
    y = lax.rem(lax.div(seq, 2), Y_CHIPS)
    z = lax.div(seq, 2 * Y_CHIPS)
    right = (seq, lax.rem(head + 1, heads))
    left = (seq, lax.rem(head + heads - 1, heads))
    other_core = (seq + 1 - 2 * core, head)
    inner = y + core * (z - y)
    outer = z + core * (y - z)
    inner_step = 2 + core * (2 * Y_CHIPS - 2)
    outer_step = 2 * Y_CHIPS - core * (2 * Y_CHIPS - 2)
    ring = z_chips

    def inner_peer(j):
        return (seq + (lax.rem(inner + j, ring) - inner) * inner_step, head)

    def outer_peer(j):
        return (seq + (lax.rem(outer + j, ring) - outer) * outer_step, head)

    loads = [
        pltpu.make_async_copy(act_hbm, act, load_sem.at[0]),
        pltpu.make_async_copy(stale_hbm, stale, load_sem.at[1]),
        pltpu.make_async_copy(wq_hbm, wq, load_sem.at[2]),
        pltpu.make_async_copy(wo_hbm, wo, load_sem.at[3]),
    ]
    for load in loads:
        load.start()

    bits = seq_count.bit_length() - 1
    y_bits = tuple(range(1, Y_CHIPS.bit_length()))
    z_bits = tuple(range(Y_CHIPS.bit_length(), bits))
    orders = (y_bits + z_bits + (0,), z_bits + y_bits + (0,))
    streams = [(1, orders[0]), (-1, orders[0]), (1, orders[1]), (-1, orders[1])]
    stream_rows = rows // len(streams)

    def at_distance(by):
        return (lax.rem(seq + by + seq_count, seq_count), head)

    barrier = pltpu.get_barrier_semaphore()
    peers = [left, right, other_core]
    peers += [inner_peer(j) for j in range(1, ring)]
    peers += [outer_peer(j) for j in range(1, ring)]
    peers += [at_distance(1 << k) for k in range(bits)]
    peers += [at_distance(-(1 << k)) for k in range(bits - 1)]
    for peer in peers:
        pl.semaphore_signal(barrier, inc=1, device_id=peer, device_id_type=MESH)
    loads[0].wait()
    in_order = jnp.where(owner_slot[0] == 0, 1.0, 0.0).astype(F32)
    owner_1 = jnp.where(owner_slot[0] == 0, owners[1], owners[0])
    offset = lax.rem(owner_1 - seq + seq_count, seq_count)
    lower, upper = act[0:rows, :].astype(F32), act[rows:, :].astype(F32)
    moving[0:rows, :] = (lower * in_order + upper * (1.0 - in_order)).astype(BF16)
    moving[rows:, :] = (upper * in_order + lower * (1.0 - in_order)).astype(BF16)
    pl.semaphore_wait(barrier, len(peers))

    def remote(src, dst, send, recv, peer):
        return pltpu.make_async_remote_copy(
            src_ref=src,
            dst_ref=dst,
            send_sem=send,
            recv_sem=recv,
            device_id=peer,
            device_id_type=MESH,
        )

    def go_home(c):
        part = pl.ds(c * CHUNK, CHUNK)
        return remote(
            moving.at[part],
            xg.at[0, part],
            home_send.at[c],
            home_recv.at[c],
            at_distance(-1),
        )

    def stride(st, stage):
        sign, order = streams[st]
        if stage == 0:
            src = moving.at[pl.ds(rows + st * stream_rows, stream_rows)]
        else:
            src = landing.at[stage - 1, st]
        return remote(
            src,
            landing.at[stage, st],
            move_send.at[stage, st],
            move_recv.at[stage, st],
            at_distance(sign * (1 << order[stage])),
        )

    def service(stage):
        for st, (sign, order) in enumerate(streams):
            stride(st, stage).wait_recv()
            by = offset if sign > 0 else lax.rem(seq_count - offset, seq_count)
            taking = lax.rem(lax.div(by, 1 << order[stage]), 2).astype(F32)
            if stage == 0:
                kept = moving[pl.ds(rows + st * stream_rows, stream_rows), :]
            else:
                kept = landing[stage - 1, st]
            new = landing[stage, st].astype(F32) * taking + kept.astype(F32) * (1.0 - taking)
            if stage + 1 < bits:
                landing[stage, st] = new.astype(BF16)
                stride(st, stage + 1).start()
            else:
                xg[0, pl.ds(rows + st * stream_rows, stream_rows), :] = new.astype(BF16)

    def direct(c, way):
        peer, slot = ((right, 1), (left, 3))[way]
        part = pl.ds(c * CHUNK, CHUNK)
        return remote(
            xg.at[0, part], xg.at[slot, part], x_send.at[way, c], x_recv.at[way, c], peer
        )

    def forward(c, way):
        peer, slot = ((right, 1), (left, 3))[way]
        part = pl.ds(pl.multiple_of(c * CHUNK + way * half, half), half)
        return remote(
            xg.at[slot, part],
            xg.at[2, part],
            x_send.at[2 + way, c],
            x_recv.at[2 + way, c],
            peer,
        )

    for c in range(per_window):
        go_home(c).start()
    for st in range(len(streams)):
        stride(st, 0).start()

    loads[1].wait()
    stage[...] = jnp.zeros_like(stage)
    row_ids = lax.broadcasted_iota(jnp.int32, (rows, width), 0)
    for kind in range(2):
        for w in range(2):
            count = counts[w]
            part = stale[kind, pl.ds(w * rows, rows), :].astype(F32)
            part = jnp.where(row_ids < count, part, 0.0)
            mean = jnp.sum(part, axis=0, keepdims=True) / count.astype(F32)
            for t in range(pairs):
                at = (kind * 2 + w) * pairs + t
                stage[pl.ds(at, 1), :] = mean[:, t * PAIR : (t + 1) * PAIR]
    pool[core, outer, inner] = stage[...].astype(BF16)

    def inner_copy(j, which):
        ref = pool.at[core, outer, which]
        return remote(ref, ref, pool_send.at[j - 1], pool_recv.at[j - 1], inner_peer(j))

    def outer_copy(j, which):
        ref = pool.at[core, which]
        at = ring + j - 2
        return remote(ref, ref, pool_send.at[at], pool_recv.at[at], outer_peer(j))

    def core_copy(which):
        ref = pool.at[which]
        at = 2 * ring - 2
        return remote(ref, ref, pool_send.at[at], pool_recv.at[at], other_core)

    for j in range(1, ring):
        inner_copy(j, inner).start()

    for c in range(per_window):
        go_home(c).wait_recv()
        for way in range(2):
            direct(c, way).start()
    service(0)

    lanes = lax.broadcasted_iota(jnp.int32, (1, PAIR), 1)
    keep = [
        jnp.where(lanes < HEAD_DIM, 1.0, 0.0),
        jnp.where(lanes < HEAD_DIM, 0.0, 1.0),
    ]

    def lay_out(at, p, key, value):
        for which in range(2):
            part = pl.ds(which * rows, rows)
            kcat[at, p, part, :] = (key * keep[which]).astype(BF16)
            vaug[at, p, part, 0:PAIR] = (value * keep[which]).astype(BF16)
            vaug[at, p, part, PAIR : 2 * PAIR] = jnp.broadcast_to(
                keep[which], (rows, PAIR)
            ).astype(BF16)

    for w in range(2):
        for p in range(pairs):
            cols = slice(p * PAIR, (p + 1) * PAIR)
            lay_out(
                w,
                p,
                stale[0, pl.ds(w * rows, rows), cols].astype(F32),
                stale[1, pl.ds(w * rows, rows), cols].astype(F32),
            )

    def pass_on(c):
        for way in range(2):
            direct(c, way).wait_recv()
            forward(c, way).start()

    def opp_copy(c, way):
        peer = (right, left)[way]
        dst = (in_opp_left, in_opp_right)[way]
        part = pl.ds(way * half, half)
        return remote(
            p_opp.at[c, part], dst.at[c], rs_send.at[way, c], rs_recv.at[way, c], peer
        )

    def share_copy(c, way, piece):
        peer = (right, left)[way]
        src = (p_right, p_left)[way]
        dst = (in_left, in_right)[way]
        part = pl.ds(piece * half, half)
        at = 2 + 2 * way + piece
        return remote(
            src.at[c, part], dst.at[c, part], rs_send.at[at, c], rs_recv.at[at, c], peer
        )

    def relay(c):
        for way in range(2):
            opp_copy(c, way).wait_recv()
            src = (p_right, p_left)[way]
            add = (in_opp_left, in_opp_right)[way]
            part = pl.ds(way * half, half)
            src[c, part, :] = (src[c, part, :].astype(F32) + add[c].astype(F32)).astype(BF16)
            share_copy(c, way, way).start()

    def softmax_out(at, p, query, bias):
        scores = lax.dot_general(
            query, kcat[at, p], (((1,), (1,)), ((), ())), preferred_element_type=F32
        )
        parts = []
        for which in range(2):
            part = scores[:, which * rows : (which + 1) * rows]
            if bias is not None:
                part = part + bias
            top = jnp.max(part, axis=1, keepdims=True)
            parts.append(jnp.exp(part - top).astype(BF16))
        both = jnp.dot(
            jnp.concatenate(parts, axis=1), vaug[at, p], preferred_element_type=F32
        )
        return both[:, 0:PAIR] / both[:, PAIR : 2 * PAIR]

    def project_queries(w):
        here = slice(w * rows, (w + 1) * rows)
        for c in range(w * per_window, (w + 1) * per_window):
            for way in range(2):
                forward(c, way).wait_recv()
        query = None
        for r in range(4):
            source = lax.rem(head + heads - r, heads)
            w_rows = pl.ds(pl.multiple_of(source * width, width), width)
            term = jnp.dot(xg[r, here, :], wq[w_rows, :], preferred_element_type=F32)
            query = term if query is None else query + term
        q_s[here, :] = (query.astype(BF16).astype(F32) * HEAD_DIM ** (-0.5)).astype(BF16)

    slots = lax.broadcasted_iota(jnp.int32, (1, rows), 1)

    def fine_part(w, p, here):
        bias = jnp.where(slots < counts[w], 0.0, -1e30)
        return softmax_out(w, p, q_s[here, p * PAIR : (p + 1) * PAIR], bias)

    def coarse_part(p, here):
        return softmax_out(2, p, q_s[here, p * PAIR : (p + 1) * PAIR], None)

    def project_out(c):
        here = slice(c * CHUNK, (c + 1) * CHUNK)

        def project(r):
            target = lax.rem(head + r, heads)
            cols = pl.ds(pl.multiple_of(target * width, PAIR), width)
            return jnp.dot(
                att_s[here, :], wo[:, cols], preferred_element_type=F32
            ).astype(BF16)

        p_opp[c] = project(2)
        opp_copy(c, 0).start()
        opp_copy(c, 1).start()
        p_right[c] = project(1)
        share_copy(c, 0, 1).start()
        p_left[c] = project(3)
        share_copy(c, 1, 0).start()
        p_own[c] = project(0)

    for j in range(1, ring):
        inner_copy(j, lax.rem(inner + ring - j, ring)).wait_recv()
    for j in range(1, ring):
        outer_copy(j, outer).start()
    service(1)
    pass_on(0)
    pass_on(1)
    service(2)
    for load in loads[2:]:
        load.wait()
    project_queries(0)
    service(3)

    for j in range(1, ring):
        outer_copy(j, lax.rem(outer + ring - j, ring)).wait_recv()
    core_copy(core).start()

    window_0 = slice(0, rows)
    for p in range(pairs):
        fine_s[:, p * PAIR : (p + 1) * PAIR] = fine_part(0, p, window_0)
    service(4)

    core_copy(1 - core).wait_recv()
    for i in range(2):
        for j in range(ring):
            at = (i * ring + j) * ring * 16
            pool_wide[pl.ds(at, ring * 16), :] = (
                pool[i, j].reshape(ring * 16, PAIR).astype(F32)
            )
    for p in range(pairs):
        pooled = []
        for kind in range(2):
            pieces = [
                pool_wide[pl.ds((kind * 2 + w) * pairs + p, seq_count, stride=16), :]
                for w in range(2)
            ]
            pooled.append(jnp.concatenate(pieces, axis=0))
        lay_out(2, p, pooled[0], pooled[1])
    service(5)

    def coarse_chunk(c):
        here = slice(c * CHUNK, (c + 1) * CHUNK)
        for p in range(pairs):
            cols = slice(p * PAIR, (p + 1) * PAIR)
            att_s[here, cols] = (fine_s[here, cols] + coarse_part(p, here)).astype(BF16)
        project_out(c)

    coarse_chunk(0)
    service(6)
    for c in range(per_window, chunks):
        for way in range(2):
            direct(c, way).start()
    coarse_chunk(1)
    relay(0)
    relay(1)
    for c in range(per_window, chunks):
        pass_on(c)
    project_queries(1)
    for c in range(per_window, chunks):
        here = slice(c * CHUNK, (c + 1) * CHUNK)
        for p in range(pairs):
            cols = slice(p * PAIR, (p + 1) * PAIR)
            att_s[here, cols] = (fine_part(1, p, here) + coarse_part(p, here)).astype(BF16)
        project_out(c)
        if c > per_window:
            relay(c - 1)
    relay(chunks - 1)

    def finish(c, carry):
        for way in range(2):
            for piece in range(2):
                share_copy(c, way, piece).wait_recv()
        here = pl.ds(pl.multiple_of(c * CHUNK, CHUNK), CHUNK)
        projected = (
            p_own[c].astype(F32) + in_left[c].astype(F32) + in_right[c].astype(F32)
        )
        out[here, :] = (xg[0, here, :].astype(F32) + projected).astype(BF16)
        return carry

    lax.fori_loop(0, chunks, finish, 0)

    for c in range(per_window):
        go_home(c).wait_send()
    for st in range(len(streams)):
        for at in range(bits):
            stride(st, at).wait_send()
    for c in range(chunks):
        for way in range(2):
            direct(c, way).wait_send()
            forward(c, way).wait_send()
            opp_copy(c, way).wait_send()
            for piece in range(2):
                share_copy(c, way, piece).wait_send()
    for j in range(1, ring):
        inner_copy(j, inner).wait_send()
        outer_copy(j, outer).wait_send()
    core_copy(core).wait_send()


def on_device(activations, owners, owner_slot, counts, stale_pairs, w_query, w_out):
    seq_count = lax.axis_size("seq")
    total, width = activations.shape
    rows = total // owners.shape[0]
    chunks = total // CHUNK
    half = CHUNK // 2
    pairs = width // PAIR
    ring = Y_CHIPS
    bits = seq_count.bit_length() - 1
    hbm = pl.BlockSpec(memory_space=pl.ANY)
    dma = pltpu.SemaphoreType.DMA
    return pl.pallas_call(
        functools.partial(attention_kernel, seq_count, rows),
        out_shape=jax.ShapeDtypeStruct((total, width), BF16),
        in_specs=[pl.BlockSpec(memory_space=pltpu.SMEM)] * 3 + [hbm] * 4,
        out_specs=pl.BlockSpec(memory_space=pltpu.VMEM),
        scratch_shapes=[
            pltpu.VMEM((total, width), BF16),
            pltpu.VMEM((total, width), BF16),
            pltpu.VMEM((bits, 4, rows // 4, width), BF16),
            pltpu.VMEM((4, total, width), BF16),
            pltpu.VMEM(stale_pairs.shape, BF16),
            pltpu.VMEM(w_query.shape, BF16),
            pltpu.VMEM(w_out.shape, BF16),
            pltpu.VMEM((16, PAIR), F32),
            pltpu.VMEM((2, ring, ring, 16, PAIR), BF16),
            pltpu.VMEM((2 * ring * ring * 16, PAIR), F32),
            pltpu.VMEM((3, pairs, 2 * rows, PAIR), BF16),
            pltpu.VMEM((3, pairs, 2 * rows, 2 * PAIR), BF16),
            pltpu.VMEM((total, width), BF16),
            pltpu.VMEM((rows, width), F32),
            pltpu.VMEM((total, width), BF16),
            pltpu.VMEM((chunks, CHUNK, width), BF16),
            pltpu.VMEM((chunks, CHUNK, width), BF16),
            pltpu.VMEM((chunks, CHUNK, width), BF16),
            pltpu.VMEM((chunks, CHUNK, width), BF16),
            pltpu.VMEM((chunks, half, width), BF16),
            pltpu.VMEM((chunks, half, width), BF16),
            pltpu.VMEM((chunks, CHUNK, width), BF16),
            pltpu.VMEM((chunks, CHUNK, width), BF16),
            dma((4,)),
            dma((rows // CHUNK,)),
            dma((rows // CHUNK,)),
            dma((bits, 4)),
            dma((bits, 4)),
            dma((4, chunks)),
            dma((4, chunks)),
            dma((6, chunks)),
            dma((6, chunks)),
            dma((2 * ring - 1,)),
            dma((2 * ring - 1,)),
        ],
        compiler_params=pltpu.CompilerParams(
            collective_id=0, has_side_effects=True, vmem_limit_bytes=60 * 1024 * 1024
        ),
        name="window_attention",
    )(owners, owner_slot, counts, activations, stale_pairs, w_query, w_out)


def solution(mesh):
    placed = (
        P("seq", "head"),
        P("seq"),
        P("seq"),
        P("seq"),
        P(None, "seq", "head"),
        P(None, "head"),
        P("head", None),
    )
    return jax.shard_map(
        on_device, mesh=mesh, in_specs=placed, out_specs=P("seq", "head"), check_vma=False
    )
```

```python
import functools

import jax
import jax.numpy as jnp
from jax import lax
from jax.experimental import pallas as pl
from jax.experimental.pallas import tpu as pltpu
from jax.sharding import PartitionSpec as P

HEAD_DIM = 64
PAIR = 2 * HEAD_DIM
Y_CHIPS = 8
CHUNK = 128
MESH = pl.DeviceIdType.MESH
F32 = jnp.float32
BF16 = jnp.bfloat16


def attention_kernel(
    seq_count,
    rows,
    owners,
    owner_slot,
    counts,
    act_hbm,
    stale_hbm,
    wq_hbm,
    wo_hbm,
    out,
    act,
    moving,
    landing,
    xg,
    stale,
    wq,
    wo,
    stage,
    pool,
    pool_wide,
    kcat,
    vaug,
    q_s,
    fine_s,
    att_s,
    p_opp,
    p_right,
    p_left,
    p_own,
    in_opp_left,
    in_opp_right,
    in_left,
    in_right,
    load_sem,
    home_send,
    home_recv,
    move_send,
    move_recv,
    x_send,
    x_recv,
    rs_send,
    rs_recv,
    pool_send,
    pool_recv,
):
    width = xg.shape[2]
    total = xg.shape[1]
    chunks = total // CHUNK
    half = CHUNK // 2
    pairs = width // PAIR
    per_window = rows // CHUNK
    z_chips = seq_count // (2 * Y_CHIPS)
    seq = lax.axis_index("seq")
    head = lax.axis_index("head")
    heads = lax.axis_size("head")
    core = lax.rem(seq, 2)
    y = lax.rem(lax.div(seq, 2), Y_CHIPS)
    z = lax.div(seq, 2 * Y_CHIPS)
    right = (seq, lax.rem(head + 1, heads))
    left = (seq, lax.rem(head + heads - 1, heads))
    other_core = (seq + 1 - 2 * core, head)
    inner = y + core * (z - y)
    outer = z + core * (y - z)
    inner_step = 2 + core * (2 * Y_CHIPS - 2)
    outer_step = 2 * Y_CHIPS - core * (2 * Y_CHIPS - 2)
    ring = z_chips

    def inner_peer(j):
        return (seq + (lax.rem(inner + j, ring) - inner) * inner_step, head)

    def outer_peer(j):
        return (seq + (lax.rem(outer + j, ring) - outer) * outer_step, head)

    loads = [
        pltpu.make_async_copy(act_hbm, act, load_sem.at[0]),
        pltpu.make_async_copy(stale_hbm, stale, load_sem.at[1]),
        pltpu.make_async_copy(wq_hbm, wq, load_sem.at[2]),
        pltpu.make_async_copy(wo_hbm, wo, load_sem.at[3]),
    ]
    for load in loads:
        load.start()

    plane = 2 * Y_CHIPS
    orders = ((2, 6, plane, 3 * plane, 1), (plane, 3 * plane, 2, 6, 1))
    stages = len(orders[0])
    stream_rows = CHUNK // 2

    def at_distance(by):
        return (lax.rem(seq + by + seq_count, seq_count), head)

    barrier = pltpu.get_barrier_semaphore()
    peers = [left, right, other_core]
    peers += [inner_peer(j) for j in range(1, ring)]
    peers += [outer_peer(j) for j in range(1, ring)]
    peers += [at_distance(sign * by) for by in orders[0] for sign in (1, -1)]
    for peer in peers:
        pl.semaphore_signal(barrier, inc=1, device_id=peer, device_id_type=MESH)
    loads[0].wait()
    in_order = jnp.where(owner_slot[0] == 0, 1.0, 0.0).astype(F32)
    owner_1 = jnp.where(owner_slot[0] == 0, owners[1], owners[0])
    offset = lax.rem(owner_1 - seq + seq_count, seq_count)
    y_part = lax.rem(lax.div(offset, 2) + 4, ring)
    z_part = lax.rem(lax.div(offset + ring, plane) + 4, ring)
    digits = {
        1: lax.rem(offset, 2),
        2: lax.rem(y_part, 3) - 1,
        6: lax.div(y_part, 3) - 1,
        plane: lax.rem(z_part, 3) - 1,
        3 * plane: lax.div(z_part, 3) - 1,
    }
    lower, upper = act[0:rows, :].astype(F32), act[rows:, :].astype(F32)
    moving[0:rows, :] = (lower * in_order + upper * (1.0 - in_order)).astype(BF16)
    moving[rows:, :] = (upper * in_order + lower * (1.0 - in_order)).astype(BF16)
    pl.semaphore_wait(barrier, len(peers))

    def remote(src, dst, send, recv, peer):
        return pltpu.make_async_remote_copy(
            src_ref=src,
            dst_ref=dst,
            send_sem=send,
            recv_sem=recv,
            device_id=peer,
            device_id_type=MESH,
        )

    def go_home(c):
        part = pl.ds(c * CHUNK, CHUNK)
        return remote(
            moving.at[part],
            xg.at[0, part],
            home_send.at[c],
            home_recv.at[c],
            at_distance(-1),
        )

    def first_row(g, st):
        return rows + g * CHUNK + st * stream_rows

    def ways(stage):
        return 1 if orders[0][stage] == 1 else 2

    def stride(stage, g, st, way):
        if stage == 0:
            src = moving.at[pl.ds(first_row(g, st), stream_rows)]
        else:
            src = landing.at[stage - 1, g, st, 0]
        return remote(
            src,
            landing.at[stage, g, st, way],
            move_send.at[stage, g, st, way],
            move_recv.at[stage, g, st, way],
            at_distance((1 - 2 * way) * orders[st][stage]),
        )

    def service(stage, g):
        for st in range(2):
            digit = digits[orders[st][stage]]
            if stage == 0:
                new = moving[pl.ds(first_row(g, st), stream_rows), :].astype(F32)
            else:
                new = landing[stage - 1, g, st, 0].astype(F32)
            new = new * (digit == 0).astype(F32)
            for way in range(ways(stage)):
                stride(stage, g, st, way).wait_recv()
                taking = (digit == 1 - 2 * way).astype(F32)
                new = new + landing[stage, g, st, way].astype(F32) * taking
            if stage + 1 < stages:
                landing[stage, g, st, 0] = new.astype(BF16)
                for way in range(ways(stage + 1)):
                    stride(stage + 1, g, st, way).start()
            else:
                xg[0, pl.ds(first_row(g, st), stream_rows), :] = new.astype(BF16)
        if stage + 1 == stages:
            for way in range(2):
                direct(per_window + g, way).start()

    def direct(c, way):
        peer, slot = ((right, 1), (left, 3))[way]
        part = pl.ds(c * CHUNK, CHUNK)
        return remote(
            xg.at[0, part], xg.at[slot, part], x_send.at[way, c], x_recv.at[way, c], peer
        )

    def forward(c, way):
        peer, slot = ((right, 1), (left, 3))[way]
        part = pl.ds(pl.multiple_of(c * CHUNK + way * half, half), half)
        return remote(
            xg.at[slot, part],
            xg.at[2, part],
            x_send.at[2 + way, c],
            x_recv.at[2 + way, c],
            peer,
        )

    for c in range(per_window):
        go_home(c).start()
    for g in range(per_window):
        for st in range(2):
            for way in range(2):
                stride(0, g, st, way).start()

    loads[1].wait()
    stage[...] = jnp.zeros_like(stage)
    row_ids = lax.broadcasted_iota(jnp.int32, (rows, width), 0)
    for kind in range(2):
        for w in range(2):
            count = counts[w]
            part = stale[kind, pl.ds(w * rows, rows), :].astype(F32)
            part = jnp.where(row_ids < count, part, 0.0)
            mean = jnp.sum(part, axis=0, keepdims=True) / count.astype(F32)
            for t in range(pairs):
                at = (kind * 2 + w) * pairs + t
                stage[pl.ds(at, 1), :] = mean[:, t * PAIR : (t + 1) * PAIR]
    pool[core, outer, inner] = stage[...].astype(BF16)

    def inner_copy(j, which):
        ref = pool.at[core, outer, which]
        return remote(ref, ref, pool_send.at[j - 1], pool_recv.at[j - 1], inner_peer(j))

    def outer_copy(j, which):
        ref = pool.at[core, which]
        at = ring + j - 2
        return remote(ref, ref, pool_send.at[at], pool_recv.at[at], outer_peer(j))

    def core_copy(which):
        ref = pool.at[which]
        at = 2 * ring - 2
        return remote(ref, ref, pool_send.at[at], pool_recv.at[at], other_core)

    for j in range(1, ring):
        inner_copy(j, inner).start()

    for c in range(per_window):
        go_home(c).wait_recv()
        for way in range(2):
            direct(c, way).start()
    service(0, 0)
    service(0, 1)

    lanes = lax.broadcasted_iota(jnp.int32, (1, PAIR), 1)
    keep = [
        jnp.where(lanes < HEAD_DIM, 1.0, 0.0),
        jnp.where(lanes < HEAD_DIM, 0.0, 1.0),
    ]

    def lay_out(at, p, key, value):
        for which in range(2):
            part = pl.ds(which * rows, rows)
            kcat[at, p, :, part] = jnp.transpose(key * keep[which]).astype(BF16)
            vaug[at, p, part, 0:PAIR] = (value * keep[which]).astype(BF16)
            vaug[at, p, part, PAIR : 2 * PAIR] = jnp.broadcast_to(
                keep[which], (rows, PAIR)
            ).astype(BF16)

    for w in range(2):
        for p in range(pairs):
            cols = slice(p * PAIR, (p + 1) * PAIR)
            lay_out(
                w,
                p,
                stale[0, pl.ds(w * rows, rows), cols].astype(F32),
                stale[1, pl.ds(w * rows, rows), cols].astype(F32),
            )

    def pass_on(c):
        for way in range(2):
            direct(c, way).wait_recv()
            forward(c, way).start()

    def opp_copy(c, way):
        peer = (right, left)[way]
        dst = (in_opp_left, in_opp_right)[way]
        part = pl.ds(way * half, half)
        return remote(
            p_opp.at[c, part], dst.at[c], rs_send.at[way, c], rs_recv.at[way, c], peer
        )

    def share_copy(c, way, piece):
        peer = (right, left)[way]
        src = (p_right, p_left)[way]
        dst = (in_left, in_right)[way]
        part = pl.ds(piece * half, half)
        at = 2 + 2 * way + piece
        return remote(
            src.at[c, part], dst.at[c, part], rs_send.at[at, c], rs_recv.at[at, c], peer
        )

    def relay(c):
        for way in range(2):
            opp_copy(c, way).wait_recv()
            src = (p_right, p_left)[way]
            add = (in_opp_left, in_opp_right)[way]
            part = pl.ds(way * half, half)
            src[c, part, :] = (src[c, part, :].astype(F32) + add[c].astype(F32)).astype(BF16)
            share_copy(c, way, way).start()

    def softmax_out(at, p, query, bias):
        scores = jnp.dot(query, kcat[at, p], preferred_element_type=F32)
        parts = []
        for which in range(2):
            part = scores[:, which * rows : (which + 1) * rows]
            if bias is not None:
                part = part + bias
            top = jnp.max(part, axis=1, keepdims=True)
            parts.append(jnp.exp(part - top).astype(BF16))
        both = jnp.dot(
            jnp.concatenate(parts, axis=1), vaug[at, p], preferred_element_type=F32
        )
        return both[:, 0:PAIR] / both[:, PAIR : 2 * PAIR]

    def project_queries(first_chunk, count):
        here = slice(first_chunk * CHUNK, (first_chunk + count) * CHUNK)
        for c in range(first_chunk, first_chunk + count):
            for way in range(2):
                forward(c, way).wait_recv()
        query = None
        for r in range(4):
            source = lax.rem(head + heads - r, heads)
            w_rows = pl.ds(pl.multiple_of(source * width, width), width)
            term = jnp.dot(xg[r, here, :], wq[w_rows, :], preferred_element_type=F32)
            query = term if query is None else query + term
        q_s[here, :] = (query.astype(BF16).astype(F32) * HEAD_DIM ** (-0.5)).astype(BF16)

    slots = lax.broadcasted_iota(jnp.int32, (1, rows), 1)

    def fine_part(w, p, here):
        bias = jnp.where(slots < counts[w], 0.0, -1e30)
        return softmax_out(w, p, q_s[here, p * PAIR : (p + 1) * PAIR], bias)

    def coarse_part(p, here):
        return softmax_out(2, p, q_s[here, p * PAIR : (p + 1) * PAIR], None)

    def project_out(c):
        here = slice(c * CHUNK, (c + 1) * CHUNK)

        def project(r):
            target = lax.rem(head + r, heads)
            cols = pl.ds(pl.multiple_of(target * width, PAIR), width)
            return jnp.dot(
                att_s[here, :], wo[:, cols], preferred_element_type=F32
            ).astype(BF16)

        p_opp[c] = project(2)
        opp_copy(c, 0).start()
        opp_copy(c, 1).start()
        p_right[c] = project(1)
        share_copy(c, 0, 1).start()
        p_left[c] = project(3)
        share_copy(c, 1, 0).start()
        p_own[c] = project(0)

    def fine_chunk(p):
        fine_s[:, p * PAIR : (p + 1) * PAIR] = fine_part(0, p, slice(0, rows))

    def coarse_chunk(c):
        here = slice(c * CHUNK, (c + 1) * CHUNK)
        for p in range(pairs):
            cols = slice(p * PAIR, (p + 1) * PAIR)
            att_s[here, cols] = (fine_s[here, cols] + coarse_part(p, here)).astype(BF16)
        project_out(c)

    def whole_chunk(c):
        project_queries(c, 1)
        here = slice(c * CHUNK, (c + 1) * CHUNK)
        for p in range(pairs):
            cols = slice(p * PAIR, (p + 1) * PAIR)
            att_s[here, cols] = (fine_part(1, p, here) + coarse_part(p, here)).astype(BF16)
        project_out(c)

    for j in range(1, ring):
        inner_copy(j, lax.rem(inner + ring - j, ring)).wait_recv()
    for j in range(1, ring):
        outer_copy(j, outer).start()
    service(1, 0)
    pass_on(0)
    service(1, 1)
    pass_on(1)
    service(2, 0)
    for j in range(1, ring):
        outer_copy(j, lax.rem(outer + ring - j, ring)).wait_recv()
    core_copy(core).start()
    service(2, 1)
    for load in loads[2:]:
        load.wait()
    project_queries(0, 2)
    service(3, 0)
    fine_chunk(0)
    service(3, 1)
    fine_chunk(1)
    service(4, 0)
    fine_chunk(2)
    service(4, 1)

    core_copy(1 - core).wait_recv()
    for i in range(2):
        for j in range(ring):
            at = (i * ring + j) * ring * 16
            pool_wide[pl.ds(at, ring * 16), :] = (
                pool[i, j].reshape(ring * 16, PAIR).astype(F32)
            )
    for p in range(pairs):
        pooled = []
        for kind in range(2):
            pieces = [
                pool_wide[pl.ds((kind * 2 + w) * pairs + p, seq_count, stride=16), :]
                for w in range(2)
            ]
            pooled.append(jnp.concatenate(pieces, axis=0))
        lay_out(2, p, pooled[0], pooled[1])

    coarse_chunk(0)
    pass_on(2)
    coarse_chunk(1)
    pass_on(3)
    relay(0)
    whole_chunk(2)
    relay(1)
    whole_chunk(3)
    relay(2)
    relay(3)

    def finish(c, carry):
        for way in range(2):
            for piece in range(2):
                share_copy(c, way, piece).wait_recv()
        here = pl.ds(pl.multiple_of(c * CHUNK, CHUNK), CHUNK)
        projected = (
            p_own[c].astype(F32) + in_left[c].astype(F32) + in_right[c].astype(F32)
        )
        out[here, :] = (xg[0, here, :].astype(F32) + projected).astype(BF16)
        return carry

    lax.fori_loop(0, chunks, finish, 0)

    for c in range(per_window):
        go_home(c).wait_send()
    for stage_at in range(stages):
        for g in range(per_window):
            for st in range(2):
                for way in range(ways(stage_at)):
                    stride(stage_at, g, st, way).wait_send()
    for c in range(chunks):
        for way in range(2):
            direct(c, way).wait_send()
            forward(c, way).wait_send()
            opp_copy(c, way).wait_send()
            for piece in range(2):
                share_copy(c, way, piece).wait_send()
    for j in range(1, ring):
        inner_copy(j, inner).wait_send()
        outer_copy(j, outer).wait_send()
    core_copy(core).wait_send()


def on_device(activations, owners, owner_slot, counts, stale_pairs, w_query, w_out):
    seq_count = lax.axis_size("seq")
    total, width = activations.shape
    rows = total // owners.shape[0]
    chunks = total // CHUNK
    half = CHUNK // 2
    pairs = width // PAIR
    ring = Y_CHIPS
    groups = rows // CHUNK
    hbm = pl.BlockSpec(memory_space=pl.ANY)
    dma = pltpu.SemaphoreType.DMA
    return pl.pallas_call(
        functools.partial(attention_kernel, seq_count, rows),
        out_shape=jax.ShapeDtypeStruct((total, width), BF16),
        in_specs=[pl.BlockSpec(memory_space=pltpu.SMEM)] * 3 + [hbm] * 4,
        out_specs=pl.BlockSpec(memory_space=pltpu.VMEM),
        scratch_shapes=[
            pltpu.VMEM((total, width), BF16),
            pltpu.VMEM((total, width), BF16),
            pltpu.VMEM((5, groups, 2, 2, CHUNK // 2, width), BF16),
            pltpu.VMEM((4, total, width), BF16),
            pltpu.VMEM(stale_pairs.shape, BF16),
            pltpu.VMEM(w_query.shape, BF16),
            pltpu.VMEM(w_out.shape, BF16),
            pltpu.VMEM((16, PAIR), F32),
            pltpu.VMEM((2, ring, ring, 16, PAIR), BF16),
            pltpu.VMEM((2 * ring * ring * 16, PAIR), F32),
            pltpu.VMEM((3, pairs, PAIR, 2 * rows), BF16),
            pltpu.VMEM((3, pairs, 2 * rows, 2 * PAIR), BF16),
            pltpu.VMEM((total, width), BF16),
            pltpu.VMEM((rows, width), F32),
            pltpu.VMEM((total, width), BF16),
            pltpu.VMEM((chunks, CHUNK, width), BF16),
            pltpu.VMEM((chunks, CHUNK, width), BF16),
            pltpu.VMEM((chunks, CHUNK, width), BF16),
            pltpu.VMEM((chunks, CHUNK, width), BF16),
            pltpu.VMEM((chunks, half, width), BF16),
            pltpu.VMEM((chunks, half, width), BF16),
            pltpu.VMEM((chunks, CHUNK, width), BF16),
            pltpu.VMEM((chunks, CHUNK, width), BF16),
            dma((4,)),
            dma((rows // CHUNK,)),
            dma((rows // CHUNK,)),
            dma((5, groups, 2, 2)),
            dma((5, groups, 2, 2)),
            dma((4, chunks)),
            dma((4, chunks)),
            dma((6, chunks)),
            dma((6, chunks)),
            dma((2 * ring - 1,)),
            dma((2 * ring - 1,)),
        ],
        compiler_params=pltpu.CompilerParams(
            collective_id=0, has_side_effects=True, vmem_limit_bytes=60 * 1024 * 1024
        ),
        name="window_attention",
    )(owners, owner_slot, counts, activations, stale_pairs, w_query, w_out)


def solution(mesh):
    placed = (
        P("seq", "head"),
        P("seq"),
        P("seq"),
        P("seq"),
        P(None, "seq", "head"),
        P(None, "head"),
        P("head", None),
    )
    return jax.shard_map(
        on_device, mesh=mesh, in_specs=placed, out_specs=P("seq", "head"), check_vma=False
    )
```

```python
import functools

import jax
import jax.numpy as jnp
from jax import lax
from jax.experimental import pallas as pl
from jax.experimental.pallas import tpu as pltpu
from jax.sharding import PartitionSpec as P

HEAD_DIM = 64
PAIR = 2 * HEAD_DIM
Y_CHIPS = 8
CHUNK = 128
MESH = pl.DeviceIdType.MESH
F32 = jnp.float32
BF16 = jnp.bfloat16


def attention_kernel(
    seq_count,
    rows,
    chunks,
    owners,
    owner_slot,
    counts,
    act_hbm,
    stale_hbm,
    wq_hbm,
    wo_hbm,
    out,
    act,
    moving,
    landing,
    xg,
    stale,
    wq,
    wo,
    stage,
    pool,
    pool_wide,
    kcat,
    vaug,
    q_s,
    att_s,
    p_opp,
    p_right,
    p_left,
    p_own,
    in_opp_left,
    in_opp_right,
    in_left,
    in_right,
    load_sem,
    home_send,
    home_recv,
    move_send,
    move_recv,
    x_send,
    x_recv,
    rs_send,
    rs_recv,
    pool_send,
    pool_recv,
):
    width = xg.shape[2]
    total = xg.shape[1]
    pairs = width // PAIR
    z_chips = seq_count // (2 * Y_CHIPS)
    seq = lax.axis_index("seq")
    head = lax.axis_index("head")
    heads = lax.axis_size("head")
    core = lax.rem(seq, 2)
    y = lax.rem(lax.div(seq, 2), Y_CHIPS)
    z = lax.div(seq, 2 * Y_CHIPS)
    right = (seq, lax.rem(head + 1, heads))
    left = (seq, lax.rem(head + heads - 1, heads))
    other_core = (seq + 1 - 2 * core, head)
    inner = y + core * (z - y)
    outer = z + core * (y - z)
    inner_step = 2 + core * (2 * Y_CHIPS - 2)
    outer_step = 2 * Y_CHIPS - core * (2 * Y_CHIPS - 2)
    ring = z_chips

    def inner_peer(j):
        return (seq + (lax.rem(inner + j, ring) - inner) * inner_step, head)

    def outer_peer(j):
        return (seq + (lax.rem(outer + j, ring) - outer) * outer_step, head)

    loads = [
        pltpu.make_async_copy(act_hbm, act, load_sem.at[0]),
        pltpu.make_async_copy(stale_hbm, stale, load_sem.at[1]),
        pltpu.make_async_copy(wq_hbm, wq, load_sem.at[2]),
        pltpu.make_async_copy(wo_hbm, wo, load_sem.at[3]),
    ]
    for load in loads:
        load.start()

    plane = 2 * Y_CHIPS
    orders = ((1, 2, 6, plane, 3 * plane), (1, plane, 3 * plane, 2, 6))
    stages = len(orders[0])
    stream_rows = CHUNK // 2

    def at_distance(by):
        return (lax.rem(seq + by + seq_count, seq_count), head)

    barrier = pltpu.get_barrier_semaphore()
    peers = [left, right, other_core]
    peers += [inner_peer(j) for j in range(1, ring)]
    peers += [outer_peer(j) for j in range(1, ring)]
    peers += [at_distance(sign * by) for by in orders[0] for sign in (1, -1)]
    for peer in peers:
        pl.semaphore_signal(barrier, inc=1, device_id=peer, device_id_type=MESH)
    loads[0].wait()
    in_order = jnp.where(owner_slot[0] == 0, 1.0, 0.0).astype(F32)
    owner_1 = jnp.where(owner_slot[0] == 0, owners[1], owners[0])
    offset = lax.rem(owner_1 - seq + seq_count, seq_count)
    y_part = lax.rem(lax.div(offset, 2) + 4, ring)
    z_part = lax.rem(lax.div(offset + ring, plane) + 4, ring)
    digits = {
        1: lax.rem(offset, 2),
        2: lax.rem(y_part, 3) - 1,
        6: lax.div(y_part, 3) - 1,
        plane: lax.rem(z_part, 3) - 1,
        3 * plane: lax.div(z_part, 3) - 1,
    }
    lower, upper = act[0:rows, :].astype(F32), act[rows:, :].astype(F32)
    moving[0:rows, :] = (lower * in_order + upper * (1.0 - in_order)).astype(BF16)
    moving[rows:, :] = (upper * in_order + lower * (1.0 - in_order)).astype(BF16)
    pl.semaphore_wait(barrier, len(peers))

    def remote(src, dst, send, recv, peer):
        return pltpu.make_async_remote_copy(
            src_ref=src,
            dst_ref=dst,
            send_sem=send,
            recv_sem=recv,
            device_id=peer,
            device_id_type=MESH,
        )

    go_home = remote(
        moving.at[pl.ds(0, rows)],
        xg.at[0, pl.ds(0, rows)],
        home_send.at[0],
        home_recv.at[0],
        at_distance(-1),
    )

    groups = len(chunks) - 1

    def all_of(c):
        start, size = chunks[c]
        return pl.ds(start, size)

    def half_of(c, piece):
        start, size = chunks[c]
        return pl.ds(start + piece * size // 2, size // 2)

    def first_row(g, st):
        return chunks[1 + g][0] + st * stream_rows

    def ways(stage):
        return 1 if orders[0][stage] == 1 else 2

    def stride(stage, g, st, way):
        if stage == 0:
            src = moving.at[pl.ds(first_row(g, st), stream_rows)]
        else:
            src = landing.at[stage - 1, g, st, 0]
        return remote(
            src,
            landing.at[stage, g, st, way],
            move_send.at[stage, g, st, way],
            move_recv.at[stage, g, st, way],
            at_distance((1 - 2 * way) * orders[st][stage]),
        )

    def service(stage, g):
        for st in range(2):
            digit = digits[orders[st][stage]]
            if stage == 0:
                new = moving[pl.ds(first_row(g, st), stream_rows), :].astype(F32)
            else:
                new = landing[stage - 1, g, st, 0].astype(F32)
            new = new * (digit == 0).astype(F32)
            for way in range(ways(stage)):
                stride(stage, g, st, way).wait_recv()
                taking = (digit == 1 - 2 * way).astype(F32)
                new = new + landing[stage, g, st, way].astype(F32) * taking
            if stage + 1 < stages:
                landing[stage, g, st, 0] = new.astype(BF16)
                for way in range(ways(stage + 1)):
                    stride(stage + 1, g, st, way).start()
            else:
                xg[0, pl.ds(first_row(g, st), stream_rows), :] = new.astype(BF16)
        if stage + 1 == stages:
            for way in range(2):
                direct(1 + g, way).start()

    def direct(c, way):
        peer, slot = ((right, 1), (left, 3))[way]
        part = all_of(c)
        return remote(
            xg.at[0, part], xg.at[slot, part], x_send.at[way, c], x_recv.at[way, c], peer
        )

    def forward(c, way):
        peer, slot = ((right, 1), (left, 3))[way]
        part = half_of(c, way)
        return remote(
            xg.at[slot, part],
            xg.at[2, part],
            x_send.at[2 + way, c],
            x_recv.at[2 + way, c],
            peer,
        )

    for g in range(groups):
        for st in range(2):
            for way in range(ways(0)):
                stride(0, g, st, way).start()
    go_home.start()

    loads[1].wait()
    stage[...] = jnp.zeros_like(stage)
    row_ids = lax.broadcasted_iota(jnp.int32, (rows, width), 0)
    for kind in range(2):
        for w in range(2):
            count = counts[w]
            part = stale[kind, pl.ds(w * rows, rows), :].astype(F32)
            part = jnp.where(row_ids < count, part, 0.0)
            mean = jnp.sum(part, axis=0, keepdims=True) / count.astype(F32)
            for t in range(pairs):
                at = (kind * 2 + w) * pairs + t
                stage[pl.ds(at, 1), :] = mean[:, t * PAIR : (t + 1) * PAIR]
    pool[core, outer, inner] = stage[...].astype(BF16)

    def inner_copy(j, which):
        ref = pool.at[core, outer, which]
        return remote(ref, ref, pool_send.at[j - 1], pool_recv.at[j - 1], inner_peer(j))

    def outer_copy(j, which):
        ref = pool.at[core, which]
        at = ring + j - 2
        return remote(ref, ref, pool_send.at[at], pool_recv.at[at], outer_peer(j))

    def core_copy(which):
        ref = pool.at[which]
        at = 2 * ring - 2
        return remote(ref, ref, pool_send.at[at], pool_recv.at[at], other_core)

    for j in range(1, ring):
        inner_copy(j, inner).start()

    for g in range(groups):
        service(0, g)
    go_home.wait_recv()
    for way in range(2):
        direct(0, way).start()

    def lay_out(at, p, key, value):
        kcat[at, p] = jnp.transpose(key).astype(BF16)
        vaug[at, p, :, 0:PAIR] = value
        vaug[at, p, :, PAIR : 2 * PAIR] = jnp.ones((rows, PAIR), BF16)

    for w in range(2):
        for p in range(pairs):
            cols = slice(p * PAIR, (p + 1) * PAIR)
            lay_out(
                w,
                p,
                stale[0, pl.ds(w * rows, rows), cols].astype(F32),
                stale[1, pl.ds(w * rows, rows), cols],
            )

    def pass_on(c):
        for way in range(2):
            direct(c, way).wait_recv()
            forward(c, way).start()

    def opp_copy(c, way):
        peer = (right, left)[way]
        dst = (in_opp_left, in_opp_right)[way]
        part = half_of(c, way)
        return remote(
            p_opp.at[part], dst.at[part], rs_send.at[way, c], rs_recv.at[way, c], peer
        )

    def share_copy(c, way, piece):
        peer = (right, left)[way]
        src = (p_right, p_left)[way]
        dst = (in_left, in_right)[way]
        part = half_of(c, piece)
        at = 2 + 2 * way + piece
        return remote(
            src.at[part], dst.at[part], rs_send.at[at, c], rs_recv.at[at, c], peer
        )

    def relay(c):
        for way in range(2):
            opp_copy(c, way).wait_recv()
            src = (p_right, p_left)[way]
            add = (in_opp_left, in_opp_right)[way]
            part = half_of(c, way)
            src[part, :] = (src[part, :].astype(F32) + add[part, :].astype(F32)).astype(BF16)
            share_copy(c, way, way).start()

    lanes = lax.broadcasted_iota(jnp.int32, (1, width), 1)
    of_first = lax.rem(lanes, PAIR) < HEAD_DIM

    def project_queries(c):
        for way in range(2):
            forward(c, way).wait_recv()
        here = all_of(c)
        query = None
        for r in range(4):
            source = lax.rem(head + heads - r, heads)
            w_rows = pl.ds(pl.multiple_of(source * width, width), width)
            term = jnp.dot(xg[r, here, :], wq[w_rows, :], preferred_element_type=F32)
            query = term if query is None else query + term
        query = query.astype(BF16).astype(F32) * HEAD_DIM ** (-0.5)
        q_s[0, here, :] = jnp.where(of_first, query, 0.0).astype(BF16)
        q_s[1, here, :] = jnp.where(of_first, 0.0, query).astype(BF16)

    slots = lax.broadcasted_iota(jnp.int32, (1, rows), 1)
    biases = [jnp.where(slots < counts[w], 0.0, -1e30) for w in range(2)]

    def softmax_out(at, p, query, bias):
        size = query.shape[0] // 2
        scores = jnp.dot(query, kcat[at, p], preferred_element_type=F32)
        if bias is not None:
            scores = scores + bias
        top = jnp.max(scores, axis=1, keepdims=True)
        weights = jnp.exp(scores - top).astype(BF16)
        both = jnp.dot(weights, vaug[at, p], preferred_element_type=F32)
        pick = of_first[:, 0:PAIR]
        summed = jnp.where(pick, both[0:size, 0:PAIR], both[size:, 0:PAIR])
        mass = jnp.where(pick, both[0:size, PAIR:], both[size:, PAIR:])
        return summed / mass

    def attend(c, w, p):
        here = all_of(c)
        cols = slice(p * PAIR, (p + 1) * PAIR)
        query = jnp.concatenate([q_s[0, here, cols], q_s[1, here, cols]], axis=0)
        fine = softmax_out(w, p, query, biases[w])
        coarse = softmax_out(2, p, query, None)
        att_s[here, cols] = (fine + coarse).astype(BF16)

    def project(c, r):
        target = lax.rem(head + r, heads)
        cols = pl.ds(pl.multiple_of(target * width, PAIR), width)
        return jnp.dot(
            att_s[all_of(c), :], wo[:, cols], preferred_element_type=F32
        ).astype(BF16)

    def project_out(c):
        p_opp[all_of(c), :] = project(c, 2)
        opp_copy(c, 0).start()
        opp_copy(c, 1).start()
        p_right[all_of(c), :] = project(c, 1)
        share_copy(c, 0, 1).start()
        p_left[all_of(c), :] = project(c, 3)
        share_copy(c, 1, 0).start()

    def project_own(c):
        p_own[all_of(c), :] = project(c, 0)

    def finish(c):
        for way in range(2):
            for piece in range(2):
                share_copy(c, way, piece).wait_recv()
        here = all_of(c)
        projected = (
            p_own[here, :].astype(F32)
            + in_left[here, :].astype(F32)
            + in_right[here, :].astype(F32)
        )
        out[here, :] = (xg[0, here, :].astype(F32) + projected).astype(BF16)

    for j in range(1, ring):
        inner_copy(j, lax.rem(inner + ring - j, ring)).wait_recv()
    for j in range(1, ring):
        outer_copy(j, outer).start()
    service(1, 0)
    service(1, 1)
    pass_on(0)
    service(2, 0)
    service(2, 1)
    for j in range(1, ring):
        outer_copy(j, lax.rem(outer + ring - j, ring)).wait_recv()
    core_copy(core).start()
    service(3, 0)
    service(3, 1)
    for load in loads[2:]:
        load.wait()
    project_queries(0)
    service(4, 0)
    service(4, 1)

    core_copy(1 - core).wait_recv()
    for i in range(2):
        for j in range(ring):
            at = (i * ring + j) * ring * 16
            pool_wide[pl.ds(at, ring * 16), :] = (
                pool[i, j].reshape(ring * 16, PAIR).astype(F32)
            )
    for p in range(pairs):
        pooled = []
        for kind in range(2):
            pieces = [
                pool_wide[pl.ds((kind * 2 + w) * pairs + p, seq_count, stride=16), :]
                for w in range(2)
            ]
            pooled.append(jnp.concatenate(pieces, axis=0))
        lay_out(2, p, pooled[0], pooled[1].astype(BF16))

    attend(0, 0, 0)
    pass_on(1)
    attend(0, 0, 1)
    pass_on(2)
    attend(0, 0, 2)
    project_out(0)

    project_queries(1)
    for p in range(pairs):
        attend(1, 1, p)
    project_out(1)
    relay(0)
    project_queries(2)
    for p in range(pairs):
        attend(2, 1, p)
    project_out(2)
    relay(1)
    for c in range(3):
        project_own(c)
    finish(0)
    relay(2)

    for j in range(1, ring):
        inner_copy(j, inner).wait_send()
        outer_copy(j, outer).wait_send()
    core_copy(core).wait_send()
    go_home.wait_send()
    for step in range(stages - 1):
        for g in range(groups):
            for st in range(2):
                for way in range(ways(step)):
                    stride(step, g, st, way).wait_send()
    for way in range(2):
        direct(0, way).wait_send()
        forward(0, way).wait_send()

    for g in range(groups):
        for st in range(2):
            for way in range(ways(stages - 1)):
                stride(stages - 1, g, st, way).wait_send()
    for c in range(1, len(chunks)):
        for way in range(2):
            direct(c, way).wait_send()
            forward(c, way).wait_send()
    finish(1)
    finish(2)
    for c in range(len(chunks)):
        for way in range(2):
            opp_copy(c, way).wait_send()
            for piece in range(2):
                share_copy(c, way, piece).wait_send()


def on_device(activations, owners, owner_slot, counts, stale_pairs, w_query, w_out):
    seq_count = lax.axis_size("seq")
    total, width = activations.shape
    rows = total // owners.shape[0]
    pairs = width // PAIR
    ring = Y_CHIPS
    chunks = [(0, rows)] + [(at, CHUNK) for at in range(rows, total, CHUNK)]
    groups = len(chunks) - 1
    hbm = pl.BlockSpec(memory_space=pl.ANY)
    dma = pltpu.SemaphoreType.DMA
    return pl.pallas_call(
        functools.partial(attention_kernel, seq_count, rows, chunks),
        out_shape=jax.ShapeDtypeStruct((total, width), BF16),
        in_specs=[pl.BlockSpec(memory_space=pltpu.SMEM)] * 3 + [hbm] * 4,
        out_specs=pl.BlockSpec(memory_space=pltpu.VMEM),
        scratch_shapes=[
            pltpu.VMEM((total, width), BF16),
            pltpu.VMEM((total, width), BF16),
            pltpu.VMEM((5, groups, 2, 2, CHUNK // 2, width), BF16),
            pltpu.VMEM((4, total, width), BF16),
            pltpu.VMEM(stale_pairs.shape, BF16),
            pltpu.VMEM(w_query.shape, BF16),
            pltpu.VMEM(w_out.shape, BF16),
            pltpu.VMEM((16, PAIR), F32),
            pltpu.VMEM((2, ring, ring, 16, PAIR), BF16),
            pltpu.VMEM((2 * ring * ring * 16, PAIR), F32),
            pltpu.VMEM((3, pairs, PAIR, rows), BF16),
            pltpu.VMEM((3, pairs, rows, 2 * PAIR), BF16),
            pltpu.VMEM((2, total, width), BF16),
        ]
        + [pltpu.VMEM((total, width), BF16)] * 9
        + [
            dma((4,)),
            dma((1,)),
            dma((1,)),
            dma((5, groups, 2, 2)),
            dma((5, groups, 2, 2)),
            dma((4, len(chunks))),
            dma((4, len(chunks))),
            dma((6, len(chunks))),
            dma((6, len(chunks))),
            dma((2 * ring - 1,)),
            dma((2 * ring - 1,)),
        ],
        compiler_params=pltpu.CompilerParams(
            collective_id=0, has_side_effects=True, vmem_limit_bytes=60 * 1024 * 1024
        ),
        name="window_attention",
    )(owners, owner_slot, counts, activations, stale_pairs, w_query, w_out)


def solution(mesh):
    placed = (
        P("seq", "head"),
        P("seq"),
        P("seq"),
        P("seq"),
        P(None, "seq", "head"),
        P(None, "head"),
        P("head", None),
    )
    return jax.shard_map(
        on_device, mesh=mesh, in_specs=placed, out_specs=P("seq", "head"), check_vma=False
    )
```

```python
import functools

import jax
import jax.numpy as jnp
from jax import lax
from jax.experimental import pallas as pl
from jax.experimental.pallas import tpu as pltpu
from jax.sharding import PartitionSpec as P

HEAD_DIM = 64
PAIR = 2 * HEAD_DIM
Y_CHIPS = 8
CHUNK = 128
MESH = pl.DeviceIdType.MESH
F32 = jnp.float32
BF16 = jnp.bfloat16


def attention_kernel(
    seq_count,
    rows,
    chunks,
    owners,
    owner_slot,
    counts,
    act_hbm,
    stale_hbm,
    wq_hbm,
    wo_hbm,
    out,
    act,
    moving,
    landing,
    xg,
    stale,
    wq,
    wo,
    stage,
    pool,
    pool_wide,
    kcat,
    vaug,
    q_s,
    att_s,
    p_opp,
    p_right,
    p_left,
    p_own,
    in_opp_left,
    in_opp_right,
    in_left,
    in_right,
    load_sem,
    home_send,
    home_recv,
    move_send,
    move_recv,
    x_send,
    x_recv,
    rs_send,
    rs_recv,
    pool_send,
    pool_recv,
):
    width = xg.shape[2]
    total = xg.shape[1]
    pairs = width // PAIR
    z_chips = seq_count // (2 * Y_CHIPS)
    seq = lax.axis_index("seq")
    head = lax.axis_index("head")
    heads = lax.axis_size("head")
    core = lax.rem(seq, 2)
    y = lax.rem(lax.div(seq, 2), Y_CHIPS)
    z = lax.div(seq, 2 * Y_CHIPS)
    right = (seq, lax.rem(head + 1, heads))
    left = (seq, lax.rem(head + heads - 1, heads))
    other_core = (seq + 1 - 2 * core, head)
    inner = y + core * (z - y)
    outer = z + core * (y - z)
    inner_step = 2 + core * (2 * Y_CHIPS - 2)
    outer_step = 2 * Y_CHIPS - core * (2 * Y_CHIPS - 2)
    ring = z_chips

    def inner_peer(j):
        return (seq + (lax.rem(inner + j, ring) - inner) * inner_step, head)

    def outer_peer(j):
        return (seq + (lax.rem(outer + j, ring) - outer) * outer_step, head)

    loads = [
        pltpu.make_async_copy(act_hbm, act, load_sem.at[0]),
        pltpu.make_async_copy(stale_hbm, stale, load_sem.at[1]),
        pltpu.make_async_copy(wq_hbm, wq, load_sem.at[2]),
        pltpu.make_async_copy(wo_hbm, wo, load_sem.at[3]),
    ]
    for load in loads:
        load.start()

    plane = 2 * Y_CHIPS
    orders = ((1, 2, 6, plane, 3 * plane), (1, plane, 3 * plane, 2, 6))
    stages = len(orders[0])
    stream_rows = CHUNK // 2

    def at_distance(by):
        return (lax.rem(seq + by + seq_count, seq_count), head)

    barrier = pltpu.get_barrier_semaphore()
    peers = [left, right, other_core]
    peers += [inner_peer(j) for j in range(1, ring)]
    peers += [outer_peer(j) for j in range(1, ring)]
    peers += [at_distance(sign * by) for by in orders[0] for sign in (1, -1)]
    for peer in peers:
        pl.semaphore_signal(barrier, inc=1, device_id=peer, device_id_type=MESH)
    loads[0].wait()
    in_order = jnp.where(owner_slot[0] == 0, 1.0, 0.0).astype(F32)
    owner_1 = jnp.where(owner_slot[0] == 0, owners[1], owners[0])
    offset = lax.rem(owner_1 - seq + seq_count, seq_count)
    odd = lax.rem(offset, 2)
    offset = offset + odd * (1 - 2 * core)
    y_part = lax.rem(lax.div(offset, 2) + 4, ring)
    z_part = lax.rem(lax.div(offset + ring, plane) + 4, ring)
    digits = {
        1: odd,
        2: lax.rem(y_part, 3) - 1,
        6: lax.div(y_part, 3) - 1,
        plane: lax.rem(z_part, 3) - 1,
        3 * plane: lax.div(z_part, 3) - 1,
    }
    lower, upper = act[0:rows, :].astype(F32), act[rows:, :].astype(F32)
    moving[0:rows, :] = (lower * in_order + upper * (1.0 - in_order)).astype(BF16)
    moving[rows:, :] = (upper * in_order + lower * (1.0 - in_order)).astype(BF16)
    pl.semaphore_wait(barrier, len(peers))

    def remote(src, dst, send, recv, peer):
        return pltpu.make_async_remote_copy(
            src_ref=src,
            dst_ref=dst,
            send_sem=send,
            recv_sem=recv,
            device_id=peer,
            device_id_type=MESH,
        )

    go_home = remote(
        moving.at[pl.ds(0, rows)],
        xg.at[0, pl.ds(0, rows)],
        home_send.at[0],
        home_recv.at[0],
        at_distance(-1),
    )

    groups = len(chunks) - 1

    def all_of(c):
        start, size = chunks[c]
        return pl.ds(start, size)

    def half_of(c, piece):
        start, size = chunks[c]
        return pl.ds(start + piece * size // 2, size // 2)

    def first_row(g, st):
        return chunks[1 + g][0] + st * stream_rows

    def ways(stage):
        return 1 if orders[0][stage] == 1 else 2

    def stride(stage, g, st, way):
        if stage == 0:
            src = moving.at[pl.ds(first_row(g, st), stream_rows)]
        else:
            src = landing.at[stage - 1, g, st, 0]
        by = orders[st][stage]
        return remote(
            src,
            landing.at[stage, g, st, way],
            move_send.at[stage, g, st, way],
            move_recv.at[stage, g, st, way],
            other_core if by == 1 else at_distance((1 - 2 * way) * by),
        )

    def service(stage, g):
        for st in range(2):
            digit = digits[orders[st][stage]]
            if stage == 0:
                new = moving[pl.ds(first_row(g, st), stream_rows), :].astype(F32)
            else:
                new = landing[stage - 1, g, st, 0].astype(F32)
            new = new * (digit == 0).astype(F32)
            for way in range(ways(stage)):
                stride(stage, g, st, way).wait_recv()
                taking = (digit == 1 - 2 * way).astype(F32)
                new = new + landing[stage, g, st, way].astype(F32) * taking
            if stage + 1 < stages:
                landing[stage, g, st, 0] = new.astype(BF16)
                for way in range(ways(stage + 1)):
                    stride(stage + 1, g, st, way).start()
            else:
                xg[0, pl.ds(first_row(g, st), stream_rows), :] = new.astype(BF16)
        if stage + 1 == stages:
            for way in range(2):
                direct(1 + g, way).start()

    def direct(c, way):
        peer, slot = ((right, 1), (left, 3))[way]
        part = all_of(c)
        return remote(
            xg.at[0, part], xg.at[slot, part], x_send.at[way, c], x_recv.at[way, c], peer
        )

    def forward(c, way):
        peer, slot = ((right, 1), (left, 3))[way]
        part = half_of(c, way)
        return remote(
            xg.at[slot, part],
            xg.at[2, part],
            x_send.at[2 + way, c],
            x_recv.at[2 + way, c],
            peer,
        )

    for g in range(groups):
        for st in range(2):
            for way in range(ways(0)):
                stride(0, g, st, way).start()
    loads[1].wait()
    stage[...] = jnp.zeros_like(stage)
    row_ids = lax.broadcasted_iota(jnp.int32, (rows, width), 0)
    for kind in range(2):
        for w in range(2):
            count = counts[w]
            part = stale[kind, pl.ds(w * rows, rows), :].astype(F32)
            part = jnp.where(row_ids < count, part, 0.0)
            mean = jnp.sum(part, axis=0, keepdims=True) / count.astype(F32)
            for t in range(pairs):
                at = (kind * 2 + w) * pairs + t
                stage[pl.ds(at, 1), :] = mean[:, t * PAIR : (t + 1) * PAIR]
    pool[core, outer, inner] = stage[...].astype(BF16)

    def inner_copy(j, which):
        ref = pool.at[core, outer, which]
        return remote(ref, ref, pool_send.at[j - 1], pool_recv.at[j - 1], inner_peer(j))

    def outer_copy(j, which):
        ref = pool.at[core, which]
        at = ring + j - 2
        return remote(ref, ref, pool_send.at[at], pool_recv.at[at], outer_peer(j))

    def core_copy(which):
        ref = pool.at[which]
        at = 2 * ring - 2
        return remote(ref, ref, pool_send.at[at], pool_recv.at[at], other_core)

    for j in range(1, ring):
        inner_copy(j, inner).start()

    for g in range(groups):
        service(0, g)
    go_home.start()

    def lay_out(at, p, key, value):
        kcat[at, p] = jnp.transpose(key).astype(BF16)
        vaug[at, p, :, 0:PAIR] = value
        vaug[at, p, :, PAIR : 2 * PAIR] = jnp.ones((rows, PAIR), BF16)

    for w in range(2):
        for p in range(pairs):
            cols = slice(p * PAIR, (p + 1) * PAIR)
            lay_out(
                w,
                p,
                stale[0, pl.ds(w * rows, rows), cols].astype(F32),
                stale[1, pl.ds(w * rows, rows), cols],
            )

    def pass_on(c):
        for way in range(2):
            direct(c, way).wait_recv()
            forward(c, way).start()

    def opp_copy(c, way):
        peer = (right, left)[way]
        dst = (in_opp_left, in_opp_right)[way]
        part = half_of(c, way)
        return remote(
            p_opp.at[part], dst.at[part], rs_send.at[way, c], rs_recv.at[way, c], peer
        )

    def share_copy(c, way, piece):
        peer = (right, left)[way]
        src = (p_right, p_left)[way]
        dst = (in_left, in_right)[way]
        part = half_of(c, piece)
        at = 2 + 2 * way + piece
        return remote(
            src.at[part], dst.at[part], rs_send.at[at, c], rs_recv.at[at, c], peer
        )

    def relay(c):
        for way in range(2):
            opp_copy(c, way).wait_recv()
            src = (p_right, p_left)[way]
            add = (in_opp_left, in_opp_right)[way]
            part = half_of(c, way)
            src[part, :] = (src[part, :].astype(F32) + add[part, :].astype(F32)).astype(BF16)
            share_copy(c, way, way).start()

    lanes = lax.broadcasted_iota(jnp.int32, (1, width), 1)
    of_first = lax.rem(lanes, PAIR) < HEAD_DIM

    def project_queries(c):
        for way in range(2):
            forward(c, way).wait_recv()
        here = all_of(c)
        query = None
        for r in range(4):
            source = lax.rem(head + heads - r, heads)
            w_rows = pl.ds(pl.multiple_of(source * width, width), width)
            term = jnp.dot(xg[r, here, :], wq[w_rows, :], preferred_element_type=F32)
            query = term if query is None else query + term
        query = query.astype(BF16).astype(F32) * HEAD_DIM ** (-0.5)
        q_s[0, here, :] = jnp.where(of_first, query, 0.0).astype(BF16)
        q_s[1, here, :] = jnp.where(of_first, 0.0, query).astype(BF16)

    slots = lax.broadcasted_iota(jnp.int32, (1, rows), 1)
    biases = [jnp.where(slots < counts[w], 0.0, -1e30) for w in range(2)]

    def softmax_out(at, p, query, bias):
        size = query.shape[0] // 2
        scores = jnp.dot(query, kcat[at, p], preferred_element_type=F32)
        if bias is not None:
            scores = scores + bias
        top = jnp.max(scores, axis=1, keepdims=True)
        weights = jnp.exp(scores - top).astype(BF16)
        both = jnp.dot(weights, vaug[at, p], preferred_element_type=F32)
        pick = of_first[:, 0:PAIR]
        summed = jnp.where(pick, both[0:size, 0:PAIR], both[size:, 0:PAIR])
        mass = jnp.where(pick, both[0:size, PAIR:], both[size:, PAIR:])
        return summed / mass

    def attend(c, w, p):
        here = all_of(c)
        cols = slice(p * PAIR, (p + 1) * PAIR)
        query = jnp.concatenate([q_s[0, here, cols], q_s[1, here, cols]], axis=0)
        fine = softmax_out(w, p, query, biases[w])
        coarse = softmax_out(2, p, query, None)
        att_s[here, cols] = (fine + coarse).astype(BF16)

    def project(c, r):
        target = lax.rem(head + r, heads)
        cols = pl.ds(pl.multiple_of(target * width, PAIR), width)
        return jnp.dot(
            att_s[all_of(c), :], wo[:, cols], preferred_element_type=F32
        ).astype(BF16)

    def project_out(c):
        p_opp[all_of(c), :] = project(c, 2)
        opp_copy(c, 0).start()
        opp_copy(c, 1).start()
        p_right[all_of(c), :] = project(c, 1)
        share_copy(c, 0, 1).start()
        p_left[all_of(c), :] = project(c, 3)
        share_copy(c, 1, 0).start()

    def project_own(c):
        p_own[all_of(c), :] = project(c, 0)

    def finish(c):
        for way in range(2):
            for piece in range(2):
                share_copy(c, way, piece).wait_recv()
        here = all_of(c)
        projected = (
            p_own[here, :].astype(F32)
            + in_left[here, :].astype(F32)
            + in_right[here, :].astype(F32)
        )
        out[here, :] = (xg[0, here, :].astype(F32) + projected).astype(BF16)

    for j in range(1, ring):
        inner_copy(j, lax.rem(inner + ring - j, ring)).wait_recv()
    for j in range(1, ring):
        outer_copy(j, outer).start()
    go_home.wait_recv()
    for way in range(2):
        direct(0, way).start()
    service(1, 0)
    service(1, 1)
    pass_on(0)
    service(2, 0)
    service(2, 1)
    for j in range(1, ring):
        outer_copy(j, lax.rem(outer + ring - j, ring)).wait_recv()
    core_copy(core).start()
    service(3, 0)
    service(3, 1)
    for load in loads[2:]:
        load.wait()
    project_queries(0)
    service(4, 0)
    service(4, 1)

    core_copy(1 - core).wait_recv()
    for i in range(2):
        for j in range(ring):
            at = (i * ring + j) * ring * 16
            pool_wide[pl.ds(at, ring * 16), :] = (
                pool[i, j].reshape(ring * 16, PAIR).astype(F32)
            )
    for p in range(pairs):
        pooled = []
        for kind in range(2):
            pieces = [
                pool_wide[pl.ds((kind * 2 + w) * pairs + p, seq_count, stride=16), :]
                for w in range(2)
            ]
            pooled.append(jnp.concatenate(pieces, axis=0))
        lay_out(2, p, pooled[0], pooled[1].astype(BF16))

    attend(0, 0, 0)
    pass_on(1)
    attend(0, 0, 1)
    pass_on(2)
    attend(0, 0, 2)
    project_out(0)

    project_queries(1)
    for p in range(pairs):
        attend(1, 1, p)
    project_out(1)
    relay(0)
    project_queries(2)
    for p in range(pairs):
        attend(2, 1, p)
    project_out(2)
    relay(1)
    for c in range(3):
        project_own(c)
    finish(0)
    relay(2)

    for j in range(1, ring):
        inner_copy(j, inner).wait_send()
        outer_copy(j, outer).wait_send()
    core_copy(core).wait_send()
    go_home.wait_send()
    for step in range(stages - 1):
        for g in range(groups):
            for st in range(2):
                for way in range(ways(step)):
                    stride(step, g, st, way).wait_send()
    for way in range(2):
        direct(0, way).wait_send()
        forward(0, way).wait_send()

    for g in range(groups):
        for st in range(2):
            for way in range(ways(stages - 1)):
                stride(stages - 1, g, st, way).wait_send()
    for c in range(1, len(chunks)):
        for way in range(2):
            direct(c, way).wait_send()
            forward(c, way).wait_send()
    finish(1)
    finish(2)
    for c in range(len(chunks)):
        for way in range(2):
            opp_copy(c, way).wait_send()
            for piece in range(2):
                share_copy(c, way, piece).wait_send()


def on_device(activations, owners, owner_slot, counts, stale_pairs, w_query, w_out):
    seq_count = lax.axis_size("seq")
    total, width = activations.shape
    rows = total // owners.shape[0]
    pairs = width // PAIR
    ring = Y_CHIPS
    chunks = [(0, rows)] + [(at, CHUNK) for at in range(rows, total, CHUNK)]
    groups = len(chunks) - 1
    hbm = pl.BlockSpec(memory_space=pl.ANY)
    dma = pltpu.SemaphoreType.DMA
    return pl.pallas_call(
        functools.partial(attention_kernel, seq_count, rows, chunks),
        out_shape=jax.ShapeDtypeStruct((total, width), BF16),
        in_specs=[pl.BlockSpec(memory_space=pltpu.SMEM)] * 3 + [hbm] * 4,
        out_specs=pl.BlockSpec(memory_space=pltpu.VMEM),
        scratch_shapes=[
            pltpu.VMEM((total, width), BF16),
            pltpu.VMEM((total, width), BF16),
            pltpu.VMEM((5, groups, 2, 2, CHUNK // 2, width), BF16),
            pltpu.VMEM((4, total, width), BF16),
            pltpu.VMEM(stale_pairs.shape, BF16),
            pltpu.VMEM(w_query.shape, BF16),
            pltpu.VMEM(w_out.shape, BF16),
            pltpu.VMEM((16, PAIR), F32),
            pltpu.VMEM((2, ring, ring, 16, PAIR), BF16),
            pltpu.VMEM((2 * ring * ring * 16, PAIR), F32),
            pltpu.VMEM((3, pairs, PAIR, rows), BF16),
            pltpu.VMEM((3, pairs, rows, 2 * PAIR), BF16),
            pltpu.VMEM((2, total, width), BF16),
        ]
        + [pltpu.VMEM((total, width), BF16)] * 9
        + [
            dma((4,)),
            dma((1,)),
            dma((1,)),
            dma((5, groups, 2, 2)),
            dma((5, groups, 2, 2)),
            dma((4, len(chunks))),
            dma((4, len(chunks))),
            dma((6, len(chunks))),
            dma((6, len(chunks))),
            dma((2 * ring - 1,)),
            dma((2 * ring - 1,)),
        ],
        compiler_params=pltpu.CompilerParams(
            collective_id=0, has_side_effects=True, vmem_limit_bytes=60 * 1024 * 1024
        ),
        name="window_attention",
    )(owners, owner_slot, counts, activations, stale_pairs, w_query, w_out)


def solution(mesh):
    placed = (
        P("seq", "head"),
        P("seq"),
        P("seq"),
        P("seq"),
        P(None, "seq", "head"),
        P(None, "head"),
        P("head", None),
    )
    return jax.shard_map(
        on_device, mesh=mesh, in_specs=placed, out_specs=P("seq", "head"), check_vma=False
    )
```

```python
import functools

import jax
import jax.numpy as jnp
from jax import lax
from jax.experimental import pallas as pl
from jax.experimental.pallas import tpu as pltpu
from jax.sharding import PartitionSpec as P

HEAD_DIM = 64
PAIR = 2 * HEAD_DIM
Y_CHIPS = 8
CHUNK = 128
MESH = pl.DeviceIdType.MESH
F32 = jnp.float32
BF16 = jnp.bfloat16


def attention_kernel(
    seq_count,
    rows,
    chunks,
    owners,
    owner_slot,
    counts,
    act_hbm,
    stale_hbm,
    wq_hbm,
    wo_hbm,
    out,
    act,
    moving,
    landing,
    xg,
    stale,
    wq,
    wo,
    stage,
    pool,
    pool_wide,
    kcat,
    vaug,
    q_s,
    att_s,
    p_opp,
    p_right,
    p_left,
    p_own,
    in_opp_left,
    in_opp_right,
    in_left,
    in_right,
    load_sem,
    home_send,
    home_recv,
    move_send,
    move_recv,
    x_send,
    x_recv,
    rs_send,
    rs_recv,
    pool_send,
    pool_recv,
):
    width = xg.shape[2]
    total = xg.shape[1]
    pairs = width // PAIR
    z_chips = seq_count // (2 * Y_CHIPS)
    seq = lax.axis_index("seq")
    head = lax.axis_index("head")
    heads = lax.axis_size("head")
    core = lax.rem(seq, 2)
    y = lax.rem(lax.div(seq, 2), Y_CHIPS)
    z = lax.div(seq, 2 * Y_CHIPS)
    right = (seq, lax.rem(head + 1, heads))
    left = (seq, lax.rem(head + heads - 1, heads))
    other_core = (seq + 1 - 2 * core, head)
    inner = y + core * (z - y)
    outer = z + core * (y - z)
    inner_step = 2 + core * (2 * Y_CHIPS - 2)
    outer_step = 2 * Y_CHIPS - core * (2 * Y_CHIPS - 2)
    ring = z_chips

    def inner_peer(j):
        return (seq + (lax.rem(inner + j, ring) - inner) * inner_step, head)

    def outer_peer(j):
        return (seq + (lax.rem(outer + j, ring) - outer) * outer_step, head)

    loads = [
        pltpu.make_async_copy(act_hbm, act, load_sem.at[0]),
        pltpu.make_async_copy(stale_hbm, stale, load_sem.at[1]),
        pltpu.make_async_copy(wq_hbm, wq, load_sem.at[2]),
        pltpu.make_async_copy(wo_hbm, wo, load_sem.at[3]),
    ]
    for load in loads:
        load.start()

    plane = 2 * Y_CHIPS
    orders = ((1, 2, 6, plane, 3 * plane), (1, plane, 3 * plane, 2, 6))
    stages = len(orders[0])
    stream_rows = CHUNK // 2

    def at_distance(by):
        return (lax.rem(seq + by + seq_count, seq_count), head)

    barrier = pltpu.get_barrier_semaphore()
    peers = [left, right, other_core]
    peers += [inner_peer(j) for j in range(1, ring)]
    peers += [outer_peer(j) for j in range(1, ring)]
    peers += [at_distance(sign * by) for by in orders[0] for sign in (1, -1)]
    for peer in peers:
        pl.semaphore_signal(barrier, inc=1, device_id=peer, device_id_type=MESH)
    loads[0].wait()
    in_order = jnp.where(owner_slot[0] == 0, 1.0, 0.0).astype(F32)
    owner_1 = jnp.where(owner_slot[0] == 0, owners[1], owners[0])
    offset = lax.rem(owner_1 - seq + seq_count, seq_count)
    odd = lax.rem(offset, 2)
    offset = offset + odd * (1 - 2 * core)
    y_part = lax.rem(lax.div(offset, 2) + 4, ring)
    z_part = lax.rem(lax.div(offset + ring, plane) + 4, ring)
    digits = {
        1: odd,
        2: lax.rem(y_part, 3) - 1,
        6: lax.div(y_part, 3) - 1,
        plane: lax.rem(z_part, 3) - 1,
        3 * plane: lax.div(z_part, 3) - 1,
    }
    lower, upper = act[0:rows, :].astype(F32), act[rows:, :].astype(F32)
    moving[0:rows, :] = (lower * in_order + upper * (1.0 - in_order)).astype(BF16)
    moving[rows:, :] = (upper * in_order + lower * (1.0 - in_order)).astype(BF16)
    pl.semaphore_wait(barrier, len(peers))

    def remote(src, dst, send, recv, peer):
        return pltpu.make_async_remote_copy(
            src_ref=src,
            dst_ref=dst,
            send_sem=send,
            recv_sem=recv,
            device_id=peer,
            device_id_type=MESH,
        )

    go_home = remote(
        moving.at[pl.ds(0, rows)],
        xg.at[0, pl.ds(0, rows)],
        home_send.at[0],
        home_recv.at[0],
        at_distance(-1),
    )

    groups = len(chunks) - 1

    def all_of(c):
        start, size = chunks[c]
        return pl.ds(start, size)

    def half_of(c, piece):
        start, size = chunks[c]
        return pl.ds(start + piece * size // 2, size // 2)

    def first_row(g, st):
        return chunks[1 + g][0] + st * stream_rows

    def ways(stage):
        return 1 if orders[0][stage] == 1 else 2

    def stride(stage, g, st, way):
        if stage == 0:
            src = moving.at[pl.ds(first_row(g, st), stream_rows)]
        else:
            src = landing.at[stage - 1, g, st, 0]
        by = orders[st][stage]
        return remote(
            src,
            landing.at[stage, g, st, way],
            move_send.at[stage, g, st, way],
            move_recv.at[stage, g, st, way],
            other_core if by == 1 else at_distance((1 - 2 * way) * by),
        )

    def service(stage, g):
        for st in range(2):
            digit = digits[orders[st][stage]]
            if stage == 0:
                new = moving[pl.ds(first_row(g, st), stream_rows), :].astype(F32)
            else:
                new = landing[stage - 1, g, st, 0].astype(F32)
            new = new * (digit == 0).astype(F32)
            for way in range(ways(stage)):
                stride(stage, g, st, way).wait_recv()
                taking = (digit == 1 - 2 * way).astype(F32)
                new = new + landing[stage, g, st, way].astype(F32) * taking
            if stage + 1 < stages:
                landing[stage, g, st, 0] = new.astype(BF16)
                for way in range(ways(stage + 1)):
                    stride(stage + 1, g, st, way).start()
            else:
                xg[0, pl.ds(first_row(g, st), stream_rows), :] = new.astype(BF16)
        if stage + 1 == stages:
            for way in range(2):
                direct(1 + g, way).start()

    def direct(c, way):
        peer, slot = ((right, 1), (left, 3))[way]
        part = all_of(c)
        return remote(
            xg.at[0, part], xg.at[slot, part], x_send.at[way, c], x_recv.at[way, c], peer
        )

    def forward(c, way):
        peer, slot = ((right, 1), (left, 3))[way]
        part = half_of(c, way)
        return remote(
            xg.at[slot, part],
            xg.at[2, part],
            x_send.at[2 + way, c],
            x_recv.at[2 + way, c],
            peer,
        )

    for g in range(groups):
        for st in range(2):
            for way in range(ways(0)):
                stride(0, g, st, way).start()
    loads[1].wait()
    stage[...] = jnp.zeros_like(stage)
    row_ids = lax.broadcasted_iota(jnp.int32, (rows, width), 0)
    for kind in range(2):
        for w in range(2):
            count = counts[w]
            part = stale[kind, pl.ds(w * rows, rows), :].astype(F32)
            part = jnp.where(row_ids < count, part, 0.0)
            mean = jnp.sum(part, axis=0, keepdims=True) / count.astype(F32)
            for t in range(pairs):
                at = (kind * 2 + w) * pairs + t
                stage[pl.ds(at, 1), :] = mean[:, t * PAIR : (t + 1) * PAIR]
    pool[core, outer, inner] = stage[...].astype(BF16)

    def inner_copy(j, which):
        ref = pool.at[core, outer, which]
        return remote(ref, ref, pool_send.at[j - 1], pool_recv.at[j - 1], inner_peer(j))

    def outer_copy(j, which):
        ref = pool.at[core, which]
        at = ring + j - 2
        return remote(ref, ref, pool_send.at[at], pool_recv.at[at], outer_peer(j))

    def core_copy(which):
        ref = pool.at[which]
        at = 2 * ring - 2
        return remote(ref, ref, pool_send.at[at], pool_recv.at[at], other_core)

    for j in range(1, ring):
        inner_copy(j, inner).start()

    for g in range(groups):
        service(0, g)
    go_home.start()

    def lay_out(at, p, key, value):
        kcat[at, p] = jnp.transpose(key).astype(BF16)
        vaug[at, p, :, 0:PAIR] = value
        vaug[at, p, :, PAIR : 2 * PAIR] = jnp.ones((rows, PAIR), BF16)

    for w in range(2):
        for p in range(pairs):
            cols = slice(p * PAIR, (p + 1) * PAIR)
            lay_out(
                w,
                p,
                stale[0, pl.ds(w * rows, rows), cols].astype(F32),
                stale[1, pl.ds(w * rows, rows), cols],
            )

    def pass_on(c):
        for way in range(2):
            direct(c, way).wait_recv()
            forward(c, way).start()

    def opp_copy(c, way):
        peer = (right, left)[way]
        dst = (in_opp_left, in_opp_right)[way]
        part = half_of(c, way)
        return remote(
            p_opp.at[part], dst.at[part], rs_send.at[way, c], rs_recv.at[way, c], peer
        )

    def share_copy(c, way, piece):
        peer = (right, left)[way]
        src = (p_right, p_left)[way]
        dst = (in_left, in_right)[way]
        part = half_of(c, piece)
        at = 2 + 2 * way + piece
        return remote(
            src.at[part], dst.at[part], rs_send.at[at, c], rs_recv.at[at, c], peer
        )

    def relay(c):
        for way in range(2):
            opp_copy(c, way).wait_recv()
            src = (p_right, p_left)[way]
            add = (in_opp_left, in_opp_right)[way]
            part = half_of(c, way)
            src[part, :] = (src[part, :].astype(F32) + add[part, :].astype(F32)).astype(BF16)
            share_copy(c, way, way).start()

    lanes = lax.broadcasted_iota(jnp.int32, (1, width), 1)
    of_first = lax.rem(lanes, PAIR) < HEAD_DIM

    def project_queries(c):
        for way in range(2):
            forward(c, way).wait_recv()
        here = all_of(c)
        query = None
        for r in range(4):
            source = lax.rem(head + heads - r, heads)
            w_rows = pl.ds(pl.multiple_of(source * width, width), width)
            term = jnp.dot(xg[r, here, :], wq[w_rows, :], preferred_element_type=F32)
            query = term if query is None else query + term
        query = query.astype(BF16).astype(F32) * HEAD_DIM ** (-0.5)
        q_s[0, here, :] = jnp.where(of_first, query, 0.0).astype(BF16)
        q_s[1, here, :] = jnp.where(of_first, 0.0, query).astype(BF16)

    slots = lax.broadcasted_iota(jnp.int32, (1, rows), 1)
    biases = [jnp.where(slots < counts[w], 0.0, -1e30) for w in range(2)]

    def softmax_out(at, p, query, bias):
        size = query.shape[0] // 2
        scores = jnp.dot(query, kcat[at, p], preferred_element_type=F32)
        if bias is not None:
            scores = scores + bias
        top = jnp.max(scores, axis=1, keepdims=True)
        weights = jnp.exp(scores - top).astype(BF16)
        both = jnp.dot(weights, vaug[at, p], preferred_element_type=F32)
        pick = of_first[:, 0:PAIR]
        summed = jnp.where(pick, both[0:size, 0:PAIR], both[size:, 0:PAIR])
        mass = jnp.where(pick, both[0:size, PAIR:], both[size:, PAIR:])
        return summed / mass

    def attend(c, w, p):
        here = all_of(c)
        cols = slice(p * PAIR, (p + 1) * PAIR)
        query = jnp.concatenate([q_s[0, here, cols], q_s[1, here, cols]], axis=0)
        fine = softmax_out(w, p, query, biases[w])
        coarse = softmax_out(2, p, query, None)
        att_s[here, cols] = (fine + coarse).astype(BF16)

    def project(c, r):
        target = lax.rem(head + r, heads)
        cols = pl.ds(pl.multiple_of(target * width, PAIR), width)
        return jnp.dot(
            att_s[all_of(c), :], wo[:, cols], preferred_element_type=F32
        ).astype(BF16)

    def project_out(c):
        p_opp[all_of(c), :] = project(c, 2)
        opp_copy(c, 0).start()
        opp_copy(c, 1).start()
        p_right[all_of(c), :] = project(c, 1)
        share_copy(c, 0, 1).start()
        p_left[all_of(c), :] = project(c, 3)
        share_copy(c, 1, 0).start()

    def project_own(c):
        p_own[all_of(c), :] = project(c, 0)

    def finish(c):
        for way in range(2):
            for piece in range(2):
                share_copy(c, way, piece).wait_recv()
        here = all_of(c)
        projected = (
            p_own[here, :].astype(F32)
            + in_left[here, :].astype(F32)
            + in_right[here, :].astype(F32)
        )
        out[here, :] = (xg[0, here, :].astype(F32) + projected).astype(BF16)

    for j in range(1, ring):
        inner_copy(j, lax.rem(inner + ring - j, ring)).wait_recv()
    for j in range(1, ring):
        outer_copy(j, outer).start()
    go_home.wait_recv()
    for way in range(2):
        direct(0, way).start()
    service(1, 0)
    service(1, 1)
    pass_on(0)
    service(2, 0)
    service(2, 1)
    service(3, 0)
    service(3, 1)
    for j in range(1, ring):
        outer_copy(j, lax.rem(outer + ring - j, ring)).wait_recv()
    core_copy(core).start()
    for load in loads[2:]:
        load.wait()
    project_queries(0)

    core_copy(1 - core).wait_recv()
    for i in range(2):
        for j in range(ring):
            at = (i * ring + j) * ring * 16
            pool_wide[pl.ds(at, ring * 16), :] = (
                pool[i, j].reshape(ring * 16, PAIR).astype(F32)
            )
    for p in range(pairs):
        pooled = []
        for kind in range(2):
            pieces = [
                pool_wide[pl.ds((kind * 2 + w) * pairs + p, seq_count, stride=16), :]
                for w in range(2)
            ]
            pooled.append(jnp.concatenate(pieces, axis=0))
        lay_out(2, p, pooled[0], pooled[1].astype(BF16))

    attend(0, 0, 0)
    attend(0, 0, 1)
    service(4, 0)
    attend(0, 0, 2)
    service(4, 1)
    project_out(0)
    pass_on(1)
    pass_on(2)

    project_queries(1)
    relay(0)
    for p in range(pairs):
        attend(1, 1, p)
    project_out(1)
    project_queries(2)
    for p in range(pairs):
        attend(2, 1, p)
    project_out(2)
    relay(1)
    for c in range(3):
        project_own(c)
    finish(0)
    relay(2)

    for j in range(1, ring):
        inner_copy(j, inner).wait_send()
        outer_copy(j, outer).wait_send()
    core_copy(core).wait_send()
    go_home.wait_send()
    for step in range(stages - 1):
        for g in range(groups):
            for st in range(2):
                for way in range(ways(step)):
                    stride(step, g, st, way).wait_send()
    for way in range(2):
        direct(0, way).wait_send()
        forward(0, way).wait_send()

    for g in range(groups):
        for st in range(2):
            for way in range(ways(stages - 1)):
                stride(stages - 1, g, st, way).wait_send()
    for c in range(1, len(chunks)):
        for way in range(2):
            direct(c, way).wait_send()
            forward(c, way).wait_send()
    finish(1)
    finish(2)
    for c in range(len(chunks)):
        for way in range(2):
            opp_copy(c, way).wait_send()
            for piece in range(2):
                share_copy(c, way, piece).wait_send()


def on_device(activations, owners, owner_slot, counts, stale_pairs, w_query, w_out):
    seq_count = lax.axis_size("seq")
    total, width = activations.shape
    rows = total // owners.shape[0]
    pairs = width // PAIR
    ring = Y_CHIPS
    chunks = [(0, rows)] + [(at, CHUNK) for at in range(rows, total, CHUNK)]
    groups = len(chunks) - 1
    hbm = pl.BlockSpec(memory_space=pl.ANY)
    dma = pltpu.SemaphoreType.DMA
    return pl.pallas_call(
        functools.partial(attention_kernel, seq_count, rows, chunks),
        out_shape=jax.ShapeDtypeStruct((total, width), BF16),
        in_specs=[pl.BlockSpec(memory_space=pltpu.SMEM)] * 3 + [hbm] * 4,
        out_specs=pl.BlockSpec(memory_space=pltpu.VMEM),
        scratch_shapes=[
            pltpu.VMEM((total, width), BF16),
            pltpu.VMEM((total, width), BF16),
            pltpu.VMEM((5, groups, 2, 2, CHUNK // 2, width), BF16),
            pltpu.VMEM((4, total, width), BF16),
            pltpu.VMEM(stale_pairs.shape, BF16),
            pltpu.VMEM(w_query.shape, BF16),
            pltpu.VMEM(w_out.shape, BF16),
            pltpu.VMEM((16, PAIR), F32),
            pltpu.VMEM((2, ring, ring, 16, PAIR), BF16),
            pltpu.VMEM((2 * ring * ring * 16, PAIR), F32),
            pltpu.VMEM((3, pairs, PAIR, rows), BF16),
            pltpu.VMEM((3, pairs, rows, 2 * PAIR), BF16),
            pltpu.VMEM((2, total, width), BF16),
        ]
        + [pltpu.VMEM((total, width), BF16)] * 9
        + [
            dma((4,)),
            dma((1,)),
            dma((1,)),
            dma((5, groups, 2, 2)),
            dma((5, groups, 2, 2)),
            dma((4, len(chunks))),
            dma((4, len(chunks))),
            dma((6, len(chunks))),
            dma((6, len(chunks))),
            dma((2 * ring - 1,)),
            dma((2 * ring - 1,)),
        ],
        compiler_params=pltpu.CompilerParams(
            collective_id=0, has_side_effects=True, vmem_limit_bytes=60 * 1024 * 1024
        ),
        name="window_attention",
    )(owners, owner_slot, counts, activations, stale_pairs, w_query, w_out)


def solution(mesh):
    placed = (
        P("seq", "head"),
        P("seq"),
        P("seq"),
        P("seq"),
        P(None, "seq", "head"),
        P(None, "head"),
        P("head", None),
    )
    return jax.shard_map(
        on_device, mesh=mesh, in_specs=placed, out_specs=P("seq", "head"), check_vma=False
    )
```

```python
import functools

import jax
import jax.numpy as jnp
from jax import lax
from jax.experimental import pallas as pl
from jax.experimental.pallas import tpu as pltpu
from jax.sharding import PartitionSpec as P

HEAD_DIM = 64
PAIR = 2 * HEAD_DIM
Y_CHIPS = 8
CHUNK = 128
MESH = pl.DeviceIdType.MESH
F32 = jnp.float32
BF16 = jnp.bfloat16


def attention_kernel(
    seq_count,
    rows,
    chunks,
    owners,
    owner_slot,
    counts,
    act_hbm,
    stale_hbm,
    wq_hbm,
    wo_hbm,
    out,
    act,
    moving,
    landing,
    xg,
    stale,
    wq,
    wo,
    stage,
    pool,
    pool_wide,
    kcat,
    vaug,
    q_s,
    att_s,
    p_opp,
    p_right,
    p_left,
    p_own,
    in_opp_left,
    in_opp_right,
    in_left,
    in_right,
    load_sem,
    home_send,
    home_recv,
    move_send,
    move_recv,
    x_send,
    x_recv,
    rs_send,
    rs_recv,
    pool_send,
    pool_recv,
):
    width = xg.shape[2]
    total = xg.shape[1]
    pairs = width // PAIR
    z_chips = seq_count // (2 * Y_CHIPS)
    seq = lax.axis_index("seq")
    head = lax.axis_index("head")
    heads = lax.axis_size("head")
    core = lax.rem(seq, 2)
    y = lax.rem(lax.div(seq, 2), Y_CHIPS)
    z = lax.div(seq, 2 * Y_CHIPS)
    right = (seq, lax.rem(head + 1, heads))
    left = (seq, lax.rem(head + heads - 1, heads))
    other_core = (seq + 1 - 2 * core, head)
    inner = y + core * (z - y)
    outer = z + core * (y - z)
    inner_step = 2 + core * (2 * Y_CHIPS - 2)
    outer_step = 2 * Y_CHIPS - core * (2 * Y_CHIPS - 2)
    ring = z_chips

    def inner_peer(j):
        return (seq + (lax.rem(inner + j, ring) - inner) * inner_step, head)

    def outer_peer(j):
        return (seq + (lax.rem(outer + j, ring) - outer) * outer_step, head)

    loads = [
        pltpu.make_async_copy(act_hbm, act, load_sem.at[0]),
        pltpu.make_async_copy(stale_hbm, stale, load_sem.at[1]),
        pltpu.make_async_copy(wq_hbm, wq, load_sem.at[2]),
        pltpu.make_async_copy(wo_hbm, wo, load_sem.at[3]),
    ]
    for load in loads:
        load.start()

    plane = 2 * Y_CHIPS
    orders = ((1, 2, 6, plane, 3 * plane), (1, plane, 3 * plane, 2, 6))
    stages = len(orders[0])
    stream_rows = CHUNK // 2

    def at_distance(by):
        return (lax.rem(seq + by + seq_count, seq_count), head)

    barrier = pltpu.get_barrier_semaphore()
    peers = [left, right, other_core]
    peers += [inner_peer(j) for j in range(1, ring)]
    peers += [outer_peer(j) for j in range(1, ring)]
    peers += [at_distance(sign * by) for by in orders[0] for sign in (1, -1)]
    for peer in peers:
        pl.semaphore_signal(barrier, inc=1, device_id=peer, device_id_type=MESH)
    loads[0].wait()
    in_order = jnp.where(owner_slot[0] == 0, 1.0, 0.0).astype(F32)
    owner_1 = jnp.where(owner_slot[0] == 0, owners[1], owners[0])
    offset = lax.rem(owner_1 - seq + seq_count, seq_count)
    y_part = lax.rem(lax.div(offset, 2) + 4, ring)
    z_part = lax.rem(lax.div(offset + ring, plane) + 4, ring)
    digits = {
        1: lax.rem(offset, 2),
        2: lax.rem(y_part, 3) - 1,
        6: lax.div(y_part, 3) - 1,
        plane: lax.rem(z_part, 3) - 1,
        3 * plane: lax.div(z_part, 3) - 1,
    }
    lower, upper = act[0:rows, :].astype(F32), act[rows:, :].astype(F32)
    moving[0:rows, :] = (lower * in_order + upper * (1.0 - in_order)).astype(BF16)
    moving[rows:, :] = (upper * in_order + lower * (1.0 - in_order)).astype(BF16)
    pl.semaphore_wait(barrier, len(peers))

    def remote(src, dst, send, recv, peer):
        return pltpu.make_async_remote_copy(
            src_ref=src,
            dst_ref=dst,
            send_sem=send,
            recv_sem=recv,
            device_id=peer,
            device_id_type=MESH,
        )

    go_home = remote(
        moving.at[pl.ds(0, rows)],
        xg.at[0, pl.ds(0, rows)],
        home_send.at[0],
        home_recv.at[0],
        at_distance(-1),
    )

    groups = len(chunks) - 1

    def all_of(c):
        start, size = chunks[c]
        return pl.ds(start, size)

    def half_of(c, piece):
        start, size = chunks[c]
        return pl.ds(start + piece * size // 2, size // 2)

    def first_row(g, st):
        return chunks[1 + g][0] + st * stream_rows

    def ways(stage):
        return 1 if orders[0][stage] == 1 else 2

    def stride(stage, g, st, way):
        if stage == 0:
            src = moving.at[pl.ds(first_row(g, st), stream_rows)]
        else:
            src = landing.at[stage - 1, g, st, 0]
        return remote(
            src,
            landing.at[stage, g, st, way],
            move_send.at[stage, g, st, way],
            move_recv.at[stage, g, st, way],
            at_distance((1 - 2 * way) * orders[st][stage]),
        )

    def service(stage, g):
        for st in range(2):
            digit = digits[orders[st][stage]]
            if stage == 0:
                new = moving[pl.ds(first_row(g, st), stream_rows), :].astype(F32)
            else:
                new = landing[stage - 1, g, st, 0].astype(F32)
            new = new * (digit == 0).astype(F32)
            for way in range(ways(stage)):
                stride(stage, g, st, way).wait_recv()
                taking = (digit == 1 - 2 * way).astype(F32)
                new = new + landing[stage, g, st, way].astype(F32) * taking
            if stage + 1 < stages:
                landing[stage, g, st, 0] = new.astype(BF16)
                for way in range(ways(stage + 1)):
                    stride(stage + 1, g, st, way).start()
            else:
                xg[0, pl.ds(first_row(g, st), stream_rows), :] = new.astype(BF16)
        if stage + 1 == stages:
            for way in range(2):
                direct(1 + g, way).start()

    def direct(c, way):
        peer, slot = ((right, 1), (left, 3))[way]
        part = all_of(c)
        return remote(
            xg.at[0, part], xg.at[slot, part], x_send.at[way, c], x_recv.at[way, c], peer
        )

    def forward(c, way):
        peer, slot = ((right, 1), (left, 3))[way]
        part = half_of(c, way)
        return remote(
            xg.at[slot, part],
            xg.at[2, part],
            x_send.at[2 + way, c],
            x_recv.at[2 + way, c],
            peer,
        )

    for g in range(groups):
        for st in range(2):
            for way in range(ways(0)):
                stride(0, g, st, way).start()
    go_home.start()

    loads[1].wait()
    stage[...] = jnp.zeros_like(stage)
    row_ids = lax.broadcasted_iota(jnp.int32, (rows, width), 0)
    for kind in range(2):
        for w in range(2):
            count = counts[w]
            part = stale[kind, pl.ds(w * rows, rows), :].astype(F32)
            part = jnp.where(row_ids < count, part, 0.0)
            mean = jnp.sum(part, axis=0, keepdims=True) / count.astype(F32)
            for t in range(pairs):
                at = (kind * 2 + w) * pairs + t
                stage[pl.ds(at, 1), :] = mean[:, t * PAIR : (t + 1) * PAIR]
    pool[core, outer, inner] = stage[...].astype(BF16)

    def inner_copy(j, which):
        ref = pool.at[core, outer, which]
        return remote(ref, ref, pool_send.at[j - 1], pool_recv.at[j - 1], inner_peer(j))

    def outer_copy(j, which):
        ref = pool.at[core, which]
        at = ring + j - 2
        return remote(ref, ref, pool_send.at[at], pool_recv.at[at], outer_peer(j))

    def core_copy(which):
        ref = pool.at[which]
        at = 2 * ring - 2
        return remote(ref, ref, pool_send.at[at], pool_recv.at[at], other_core)

    for j in range(1, ring):
        inner_copy(j, inner).start()

    for g in range(groups):
        service(0, g)
    go_home.wait_recv()
    for way in range(2):
        direct(0, way).start()

    def lay_out(at, p, key, value):
        kcat[at, p] = jnp.transpose(key).astype(BF16)
        vaug[at, p, :, 0:PAIR] = value
        vaug[at, p, :, PAIR : 2 * PAIR] = jnp.ones((rows, PAIR), BF16)

    for w in range(2):
        for p in range(pairs):
            cols = slice(p * PAIR, (p + 1) * PAIR)
            lay_out(
                w,
                p,
                stale[0, pl.ds(w * rows, rows), cols].astype(F32),
                stale[1, pl.ds(w * rows, rows), cols],
            )

    def pass_on(c):
        for way in range(2):
            direct(c, way).wait_recv()
            forward(c, way).start()

    def opp_copy(c, way):
        peer = (right, left)[way]
        dst = (in_opp_left, in_opp_right)[way]
        part = half_of(c, way)
        return remote(
            p_opp.at[part], dst.at[part], rs_send.at[way, c], rs_recv.at[way, c], peer
        )

    def share_copy(c, way, piece):
        peer = (right, left)[way]
        src = (p_right, p_left)[way]
        dst = (in_left, in_right)[way]
        part = half_of(c, piece)
        at = 2 + 2 * way + piece
        return remote(
            src.at[part], dst.at[part], rs_send.at[at, c], rs_recv.at[at, c], peer
        )

    def relay(c):
        for way in range(2):
            opp_copy(c, way).wait_recv()
            src = (p_right, p_left)[way]
            add = (in_opp_left, in_opp_right)[way]
            part = half_of(c, way)
            src[part, :] = (src[part, :].astype(F32) + add[part, :].astype(F32)).astype(BF16)
            share_copy(c, way, way).start()

    lanes = lax.broadcasted_iota(jnp.int32, (1, width), 1)
    of_first = lax.rem(lanes, PAIR) < HEAD_DIM

    def project_queries(c):
        for way in range(2):
            forward(c, way).wait_recv()
        here = all_of(c)
        query = None
        for r in range(4):
            source = lax.rem(head + heads - r, heads)
            w_rows = pl.ds(pl.multiple_of(source * width, width), width)
            term = jnp.dot(xg[r, here, :], wq[w_rows, :], preferred_element_type=F32)
            query = term if query is None else query + term
        query = query.astype(BF16).astype(F32) * HEAD_DIM ** (-0.5)
        q_s[0, here, :] = jnp.where(of_first, query, 0.0).astype(BF16)
        q_s[1, here, :] = jnp.where(of_first, 0.0, query).astype(BF16)

    slots = lax.broadcasted_iota(jnp.int32, (1, rows), 1)
    biases = [jnp.where(slots < counts[w], 0.0, -1e30) for w in range(2)]

    def softmax_out(at, p, query, bias):
        size = query.shape[0] // 2
        scores = jnp.dot(query, kcat[at, p], preferred_element_type=F32)
        if bias is not None:
            scores = scores + bias
        top = jnp.max(scores, axis=1, keepdims=True)
        weights = jnp.exp(scores - top).astype(BF16)
        both = jnp.dot(weights, vaug[at, p], preferred_element_type=F32)
        pick = of_first[:, 0:PAIR]
        summed = jnp.where(pick, both[0:size, 0:PAIR], both[size:, 0:PAIR])
        mass = jnp.where(pick, both[0:size, PAIR:], both[size:, PAIR:])
        return summed / mass

    def attend(c, w, p):
        here = all_of(c)
        cols = slice(p * PAIR, (p + 1) * PAIR)
        query = jnp.concatenate([q_s[0, here, cols], q_s[1, here, cols]], axis=0)
        fine = softmax_out(w, p, query, biases[w])
        coarse = softmax_out(2, p, query, None)
        att_s[here, cols] = (fine + coarse).astype(BF16)

    def project(c, r):
        target = lax.rem(head + r, heads)
        cols = pl.ds(pl.multiple_of(target * width, PAIR), width)
        return jnp.dot(
            att_s[all_of(c), :], wo[:, cols], preferred_element_type=F32
        ).astype(BF16)

    def project_out(c):
        p_opp[all_of(c), :] = project(c, 2)
        opp_copy(c, 0).start()
        opp_copy(c, 1).start()
        p_right[all_of(c), :] = project(c, 1)
        share_copy(c, 0, 1).start()
        p_left[all_of(c), :] = project(c, 3)
        share_copy(c, 1, 0).start()

    def project_own(c):
        p_own[all_of(c), :] = project(c, 0)

    def finish(c):
        for way in range(2):
            for piece in range(2):
                share_copy(c, way, piece).wait_recv()
        here = all_of(c)
        projected = (
            p_own[here, :].astype(F32)
            + in_left[here, :].astype(F32)
            + in_right[here, :].astype(F32)
        )
        out[here, :] = (xg[0, here, :].astype(F32) + projected).astype(BF16)

    for j in range(1, ring):
        inner_copy(j, lax.rem(inner + ring - j, ring)).wait_recv()
    for j in range(1, ring):
        outer_copy(j, outer).start()
    service(1, 0)
    service(1, 1)
    pass_on(0)
    service(2, 0)
    service(2, 1)
    for j in range(1, ring):
        outer_copy(j, lax.rem(outer + ring - j, ring)).wait_recv()
    core_copy(core).start()
    service(3, 0)
    service(3, 1)
    for load in loads[2:]:
        load.wait()
    project_queries(0)
    service(4, 0)
    service(4, 1)

    core_copy(1 - core).wait_recv()
    for i in range(2):
        for j in range(ring):
            at = (i * ring + j) * ring * 16
            pool_wide[pl.ds(at, ring * 16), :] = (
                pool[i, j].reshape(ring * 16, PAIR).astype(F32)
            )
    for p in range(pairs):
        pooled = []
        for kind in range(2):
            pieces = [
                pool_wide[pl.ds((kind * 2 + w) * pairs + p, seq_count, stride=16), :]
                for w in range(2)
            ]
            pooled.append(jnp.concatenate(pieces, axis=0))
        lay_out(2, p, pooled[0], pooled[1].astype(BF16))

    attend(0, 0, 0)
    pass_on(1)
    attend(0, 0, 1)
    pass_on(2)
    attend(0, 0, 2)
    project_out(0)

    project_queries(1)
    relay(0)
    for p in range(pairs):
        attend(1, 1, p)
    project_out(1)
    project_queries(2)
    for p in range(pairs):
        attend(2, 1, p)
    project_out(2)
    relay(1)
    for c in range(3):
        project_own(c)
    finish(0)
    relay(2)

    for j in range(1, ring):
        inner_copy(j, inner).wait_send()
        outer_copy(j, outer).wait_send()
    core_copy(core).wait_send()
    go_home.wait_send()
    for step in range(stages - 1):
        for g in range(groups):
            for st in range(2):
                for way in range(ways(step)):
                    stride(step, g, st, way).wait_send()
    for way in range(2):
        direct(0, way).wait_send()
        forward(0, way).wait_send()

    for g in range(groups):
        for st in range(2):
            for way in range(ways(stages - 1)):
                stride(stages - 1, g, st, way).wait_send()
    for c in range(1, len(chunks)):
        for way in range(2):
            direct(c, way).wait_send()
            forward(c, way).wait_send()
    finish(1)
    finish(2)
    for c in range(len(chunks)):
        for way in range(2):
            opp_copy(c, way).wait_send()
            for piece in range(2):
                share_copy(c, way, piece).wait_send()


def on_device(activations, owners, owner_slot, counts, stale_pairs, w_query, w_out):
    seq_count = lax.axis_size("seq")
    total, width = activations.shape
    rows = total // owners.shape[0]
    pairs = width // PAIR
    ring = Y_CHIPS
    chunks = [(0, rows)] + [(at, CHUNK) for at in range(rows, total, CHUNK)]
    groups = len(chunks) - 1
    hbm = pl.BlockSpec(memory_space=pl.ANY)
    dma = pltpu.SemaphoreType.DMA
    return pl.pallas_call(
        functools.partial(attention_kernel, seq_count, rows, chunks),
        out_shape=jax.ShapeDtypeStruct((total, width), BF16),
        in_specs=[pl.BlockSpec(memory_space=pltpu.SMEM)] * 3 + [hbm] * 4,
        out_specs=pl.BlockSpec(memory_space=pltpu.VMEM),
        scratch_shapes=[
            pltpu.VMEM((total, width), BF16),
            pltpu.VMEM((total, width), BF16),
            pltpu.VMEM((5, groups, 2, 2, CHUNK // 2, width), BF16),
            pltpu.VMEM((4, total, width), BF16),
            pltpu.VMEM(stale_pairs.shape, BF16),
            pltpu.VMEM(w_query.shape, BF16),
            pltpu.VMEM(w_out.shape, BF16),
            pltpu.VMEM((16, PAIR), F32),
            pltpu.VMEM((2, ring, ring, 16, PAIR), BF16),
            pltpu.VMEM((2 * ring * ring * 16, PAIR), F32),
            pltpu.VMEM((3, pairs, PAIR, rows), BF16),
            pltpu.VMEM((3, pairs, rows, 2 * PAIR), BF16),
            pltpu.VMEM((2, total, width), BF16),
        ]
        + [pltpu.VMEM((total, width), BF16)] * 9
        + [
            dma((4,)),
            dma((1,)),
            dma((1,)),
            dma((5, groups, 2, 2)),
            dma((5, groups, 2, 2)),
            dma((4, len(chunks))),
            dma((4, len(chunks))),
            dma((6, len(chunks))),
            dma((6, len(chunks))),
            dma((2 * ring - 1,)),
            dma((2 * ring - 1,)),
        ],
        compiler_params=pltpu.CompilerParams(
            collective_id=0, has_side_effects=True, vmem_limit_bytes=60 * 1024 * 1024
        ),
        name="window_attention",
    )(owners, owner_slot, counts, activations, stale_pairs, w_query, w_out)


def solution(mesh):
    placed = (
        P("seq", "head"),
        P("seq"),
        P("seq"),
        P("seq"),
        P(None, "seq", "head"),
        P(None, "head"),
        P("head", None),
    )
    return jax.shard_map(
        on_device, mesh=mesh, in_specs=placed, out_specs=P("seq", "head"), check_vma=False
    )
```
